32 devices in a mesh: gx: 2 (over y), gy: 4 (over z), af: 4 (over x, core).
Axes of the slice: x: 2, y: 2, z: 4, core: 2. Of those that a mesh axis runs over, the one named last changes fastest.
Arguments:
- press_matrix: float32 [8, 16, 2048], P(None, 'gx', ('gy', 'af')), may hold values from -1.5 to 1.5
- cond_matrix: float32 [8, 16, 2048], P(None, 'gx', ('gy', 'af')), may hold values from 0.05 to 0.5
- accum_matrix: float32 [8, 16, 2048], P(None, 'gx', ('gy', 'af')), may hold values from 0.5 to 2
- press_frac: float32 [128, 256], P(('gx', 'gy', 'af')), may hold values from -1.5 to 1.5
- accum_frac: float32 [128, 256], P(('gx', 'gy', 'af')), may hold values from 0.3 to 1
- trans_chain: float32 [128, 256], P(('gx', 'gy', 'af')), may hold values from 0.1 to 1
- couple_mf: float32 [128, 256], P(('gx', 'gy', 'af')), may hold values from 0.7 to 1.4
- couple_fm: float32 [128, 256], P(('gx', 'gy', 'af')), may hold values from 0.6 to 1.2
- conn_tile: int32 [128, 256], P(('gx', 'gy', 'af')), may hold values from 0 to 31, as said below
- conn_layer: int32 [128, 256], P(('gx', 'gy', 'af')), may hold values from 0 to 7
- conn_cell: int32 [128, 256], P(('gx', 'gy', 'af')), may hold values from 0 to 1023
- inter_delta: int32 [128], P(('gx', 'gy', 'af')), may hold values from 0 to 4, as said below
- inter_from: int32 [128], P(('gx', 'gy', 'af')), may hold values from 0 to 255
- inter_to: int32 [128], P(('gx', 'gy', 'af')), may hold values from 0 to 255
- inter_trans: float32 [128], P(('gx', 'gy', 'af')), may hold values from 0.5 to 2
- well_tile: int32 [32], replicated, may hold values from 0 to 31
- well_cell: int32 [32], replicated, may hold values from 0 to 1023
- well_rate: float32 [32], replicated, may hold values from -8 to 8
Outputs:
- res_matrix: float32 [8, 16, 2048], P(None, 'gx', ('gy', 'af'))
- res_fracture: float32 [128, 256], P(('gx', 'gy', 'af'))
- adj_matrix: float32 [8, 16, 2048], P(None, 'gx', ('gy', 'af'))
- adj_fracture: float32 [128, 256], P(('gx', 'gy', 'af'))
The draws below stay inside these ranges and needn't reach their ends.
Inputs may be any that keep to these rules, and one draw needn't show every extreme that they name: `conn_tile`: in each aligned run of 1024 segments (blocks k * 4 to (k + 1) * 4 - 1), at most 64 segments lie in cells of one tile; in every draw some tile holds exactly 64 segments of every such run. b + inter_delta(b) never passes the last block; the value 4 is reached.
All inputs are finite; a program needn't handle non-finite values.
Results may differ from the reference program's by a relative error of at most 0.00013.
Values sent between devices are 32-bit elements; how exact they have to be, the bound alone decides.
A program may use at most 64 MiB of HBM per device.

```python
import math
import jax
import jax.numpy as jnp
from jax import lax

CX = 8
CY = 128
NZ = 8
FB_DEV = 4
BLOCK = 256
NW = 32
ITERS = 8
NTILE = 32
NX = 16
NY = 2048
NFB = 128
SEG_DEV = 1024
CAP = 64
N_GY = 4
N_AF = 4


def draw_conn_tile(key, part):
    key_level = jax.random.fold_in(key, 11)
    key_heavy = jax.random.fold_in(key, 12)
    key_noise = jax.random.fold_in(key, 13)
    key_order = jax.random.fold_in(key, 14)
    levels = jax.random.randint(key_level, (NTILE, NTILE), 0, 4)
    heavy = jax.random.randint(key_heavy, (), 0, NTILE)
    owner_ids = jnp.arange(NTILE)
    levels = jnp.where(owner_ids[None, :] == heavy, 15, levels)
    slot_ids = jnp.arange(NTILE * CAP)
    slot_owner = slot_ids // CAP
    noise = jax.random.randint(key_noise, (NTILE, NTILE * CAP), 0, 128)
    scores = (levels[:, slot_owner] * 128 + noise) * (NTILE * CAP) + slot_ids[None, :]
    chosen = lax.top_k(scores, SEG_DEV)[1]
    owners = chosen // CAP
    owners = jax.random.permutation(key_order, owners, axis=1, independent=True)
    return owners.reshape(NFB, BLOCK).astype(jnp.int32)


def draw_inter_delta(key, part):
    raw = jax.random.randint(jax.random.fold_in(key, 23), (NFB,), 0, FB_DEV + 1)
    block_ids = jnp.arange(NFB)
    raw = jnp.where(block_ids == 0, FB_DEV, raw)
    return jnp.minimum(raw, NFB - 1 - block_ids).astype(jnp.int32)


def touch_ends(result, own_key, low, largest):
    shape = result.shape
    index_at = [jax.random.randint(jax.random.fold_in(own_key, axis), (), 0, shape[axis]) for axis in range(len(shape))]
    result = result.at[tuple(index_at)].set(low)
    longest = shape.index(max(shape))
    index_at[longest] = (index_at[longest] + 1) % shape[longest]
    return result.at[tuple(index_at)].set(largest)


def steps_of(key, dims, pieces, low, top_value):
    def one(axis_at, blocks):
        steps = jax.random.uniform(jax.random.fold_in(jax.random.fold_in(key, 6), axis_at), (blocks,), jnp.float32, low / len(pieces), top_value / len(pieces))
        return jnp.repeat(jnp.exp(steps), dims[axis_at] // blocks).reshape((-1,) + (1,) * (len(dims) - axis_at - 1))

    gain = one(*pieces[0])
    for cut in pieces[1:]:
        gain = gain * one(*cut)
    return gain


def centred(rng, shape, scale, limit, split=(), held_as=jnp.bfloat16):
    drawn = jax.random.normal(rng, shape, jnp.float32) * scale
    if len(split) > 0:
        drawn = steps_of(rng, shape, split, -0.22, 0.18) * drawn
    return jnp.clip(drawn, min=-limit, max=limit).astype(held_as)


def setup_inputs(seed: int = 0) -> dict:
    seeds = jax.random.split(jax.random.key(seed), 19)
    return {
        "press_matrix": centred(seeds[0], (NZ, NX, NY), 0.25, 1.5, ((1, 2), (2, 16)), jnp.float32),
        "cond_matrix": jnp.clip(jnp.exp(math.log(0.5) - 2.3025851 * jax.random.uniform(seeds[1], (NZ, NX, NY), jnp.float32) ** steps_of(seeds[1], (NZ, NX, NY), ((1, 2), (2, 16)), -0.2, 0.2)), 0.05, 0.5),
        "accum_matrix": jnp.clip(jnp.exp(math.log(2.0) - 1.3862944 * jax.random.uniform(seeds[2], (NZ, NX, NY), jnp.float32) ** steps_of(seeds[2], (NZ, NX, NY), ((1, 2), (2, 16)), -0.2, 0.2)), 0.5, 2.0),
        "press_frac": centred(seeds[3], (NFB, BLOCK), 0.25, 1.5, ((0, 32),), jnp.float32),
        "accum_frac": jnp.clip(jnp.exp(math.log(1.0) - 1.2039728 * jax.random.uniform(seeds[4], (NFB, BLOCK), jnp.float32) ** steps_of(seeds[4], (NFB, BLOCK), ((0, 32),), -0.2, 0.2)), 0.3, 1.0),
        "trans_chain": jnp.clip(jnp.exp(math.log(1.0) - 2.3025851 * jax.random.uniform(seeds[5], (NFB, BLOCK), jnp.float32) ** steps_of(seeds[5], (NFB, BLOCK), ((0, 32),), -0.2, 0.2)), 0.1, 1.0),
        "couple_mf": jnp.clip(jnp.exp(math.log(1.4) - 0.6931472 * jax.random.uniform(seeds[6], (NFB, BLOCK), jnp.float32) ** steps_of(seeds[6], (NFB, BLOCK), ((0, 32),), -0.2, 0.2)), 0.7, 1.4),
        "couple_fm": jnp.clip(jnp.exp(math.log(1.2) - 0.6931472 * jax.random.uniform(seeds[7], (NFB, BLOCK), jnp.float32) ** steps_of(seeds[7], (NFB, BLOCK), ((0, 32),), -0.2, 0.2)), 0.6, 1.2),
        "conn_tile": draw_conn_tile(jax.random.fold_in(seeds[18], 71), 0),
        "conn_layer": touch_ends(jax.random.randint(seeds[9], (NFB, BLOCK), 0, NZ), jax.random.fold_in(seeds[9], 1), 0, NZ - 1).astype(jnp.int32),
        "conn_cell": touch_ends(jax.random.randint(seeds[10], (NFB, BLOCK), 0, CX * CY), jax.random.fold_in(seeds[10], 1), 0, (CX * CY) - 1).astype(jnp.int32),
        "inter_delta": draw_inter_delta(jax.random.fold_in(seeds[18], 71), 0),
        "inter_from": touch_ends(jax.random.randint(seeds[12], (NFB,), 0, BLOCK), jax.random.fold_in(seeds[12], 1), 0, BLOCK - 1).astype(jnp.int32),
        "inter_to": touch_ends(jax.random.randint(seeds[13], (NFB,), 0, BLOCK), jax.random.fold_in(seeds[13], 1), 0, BLOCK - 1).astype(jnp.int32),
        "inter_trans": jnp.clip(jnp.exp(math.log(2.0) - 1.3862944 * jax.random.uniform(seeds[14], (NFB,), jnp.float32) ** steps_of(seeds[14], (NFB,), ((0, 32),), -0.2, 0.2)), 0.5, 2.0),
        "well_tile": touch_ends(jax.random.randint(seeds[15], (NW,), 0, NTILE), jax.random.fold_in(seeds[15], 1), 0, NTILE - 1).astype(jnp.int32),
        "well_cell": touch_ends(jax.random.randint(seeds[16], (NW,), 0, CX * CY), jax.random.fold_in(seeds[16], 1), 0, (CX * CY) - 1).astype(jnp.int32),
        "well_rate": centred(seeds[17], (NW,), 2.0, 8.0, (), jnp.float32),
    }


vertical_factor = 0.5


def harmonic(first, second):
    return 2.0 * first * second / (first + second)


def reference(press_matrix, cond_matrix, accum_matrix, press_frac, accum_frac, trans_chain, couple_mf, couple_fm, conn_tile, conn_layer, conn_cell, inter_delta, inter_from, inter_to, inter_trans, well_tile, well_cell, well_rate):
    tiles_y = N_GY * N_AF
    pad_x = jnp.pad(cond_matrix, ((0, 0), (1, 1), (0, 0)))
    trans_x = harmonic(pad_x[:, :-1], pad_x[:, 1:])
    pad_y = jnp.pad(cond_matrix, ((0, 0), (0, 0), (1, 1)))
    trans_y = harmonic(pad_y[:, :, :-1], pad_y[:, :, 1:])
    trans_z = vertical_factor * harmonic(cond_matrix[:-1], cond_matrix[1:])
    zero_layer = jnp.zeros((1, NX, NY), jnp.float32)
    diag_matrix = accum_matrix + trans_x[:, 1:] + trans_x[:, :-1] + trans_y[:, :, 1:] + trans_y[:, :, :-1]
    diag_matrix = diag_matrix + jnp.concatenate([trans_z, zero_layer]) + jnp.concatenate([zero_layer, trans_z])

    def stencil(field):
        field_x = jnp.pad(field, ((0, 0), (1, 1), (0, 0)))
        field_y = jnp.pad(field, ((0, 0), (0, 0), (1, 1)))
        total = trans_x[:, 1:] * field_x[:, 2:] + trans_x[:, :-1] * field_x[:, :-2]
        total = total + trans_y[:, :, 1:] * field_y[:, :, 2:] + trans_y[:, :, :-1] * field_y[:, :, :-2]
        total = total + jnp.concatenate([trans_z * field[1:], zero_layer]) + jnp.concatenate([zero_layer, trans_z * field[:-1]])
        return total

    position = jnp.arange(BLOCK)
    trans_next = jnp.where(position[None, :] < BLOCK - 1, trans_chain, 0.0)
    zero_col = jnp.zeros((NFB, 1), jnp.float32)
    trans_prev = jnp.concatenate([zero_col, trans_next[:, :-1]], axis=1)
    diag_frac = accum_frac + trans_next + trans_prev + couple_fm

    def chain(field):
        upper = jnp.concatenate([field[:, 1:], zero_col], axis=1)
        lower = jnp.concatenate([zero_col, field[:, :-1]], axis=1)
        return trans_next * upper + trans_prev * lower

    row_x = (conn_tile // tiles_y) * CX + conn_cell // CY
    col_y = (conn_tile % tiles_y) * CY + conn_cell % CY

    def gather_cells(field):
        return field[conn_layer, row_x, col_y]

    def scatter_cells(values):
        return jnp.zeros((NZ, NX, NY), jnp.float32).at[conn_layer, row_x, col_y].add(values)

    partner_row = jnp.arange(NFB, dtype=jnp.int32) + inter_delta
    from_hot = (position[None, :] == inter_from[:, None]).astype(jnp.float32)

    def forward_cross(field):
        picked = field[partner_row, inter_to]
        return from_hot * (inter_trans * picked)[:, None]

    def adjoint_cross(field):
        picked = inter_trans * jnp.sum(from_hot * field, axis=1)
        return jnp.zeros((NFB, BLOCK), jnp.float32).at[partner_row, inter_to].add(picked)

    well_x = (well_tile // tiles_y) * CX + well_cell // CY
    well_y = (well_tile % tiles_y) * CY + well_cell % CY
    source_plane = jnp.zeros((NX, NY), jnp.float32).at[well_x, well_y].add(well_rate)
    source = jnp.broadcast_to(source_plane[None], (NZ, NX, NY))

    res_matrix = diag_matrix * press_matrix - stencil(press_matrix) - scatter_cells(couple_mf * press_frac) - source
    res_fracture = diag_frac * press_frac - chain(press_frac) - couple_fm * gather_cells(press_matrix) - forward_cross(press_frac)

    adj_matrix = res_matrix / diag_matrix
    adj_fracture = res_fracture / diag_frac
    for sweep_index in range(ITERS - 1):
        image_matrix = diag_matrix * adj_matrix - stencil(adj_matrix) - scatter_cells(couple_fm * adj_fracture)
        image_fracture = diag_frac * adj_fracture - chain(adj_fracture) - couple_mf * gather_cells(adj_matrix) - adjoint_cross(adj_fracture)
        adj_matrix = adj_matrix + (res_matrix - image_matrix) / diag_matrix
        adj_fracture = adj_fracture + (res_fracture - image_fracture) / diag_frac
    return res_matrix, res_fracture, adj_matrix, adj_fracture
```

```python
import functools

import jax
import jax.numpy as jnp
from jax import lax
from jax.experimental import pallas as pl
from jax.experimental.pallas import tpu as pltpu
from jax.sharding import PartitionSpec as P

ITERS = 8
ROUNDS = ITERS + 1
SLOT = 64
MESH = pl.DeviceIdType.MESH
f32 = jnp.float32
bf16 = jnp.bfloat16


def harmonic(first, second):
    return 2.0 * first * second / (first + second)


def iota(shape, dim):
    return lax.broadcasted_iota(jnp.int32, shape, dim)


def hot(mask):
    return jnp.where(mask, 1.0, 0.0)


def pieces(values):
    high = values.astype(bf16)
    return high, (values - high.astype(f32)).astype(bf16)


def dot_nn(a, b):
    return lax.dot_general(a, b, (((1,), (0,)), ((), ())), preferred_element_type=f32)


def dot_nt(a, b):
    return lax.dot_general(a, b, (((1,), (1,)), ((), ())), preferred_element_type=f32)


def pick(table, lanes_twice, rows):
    found = dot_nn(jnp.concatenate(pieces(table), axis=1), lanes_twice)
    return jnp.sum(found * rows, axis=0, keepdims=True)


def spread(values, rows, lanes):
    count = rows.shape[0]
    both = dot_nt(jnp.concatenate(pieces(rows * values), axis=0), lanes)
    return both[:count] + both[count:]


def kernel(
    sizes,
    press_ref,
    cond_ref,
    accum_ref,
    pfrac_ref,
    afrac_ref,
    chain_ref,
    mf_ref,
    fm_ref,
    tile_ref,
    layer_ref,
    cell_ref,
    delta_ref,
    from_ref,
    to_ref,
    itrans_ref,
    wtile_ref,
    wcell_ref,
    wrate_ref,
    resm_ref,
    resf_ref,
    adjm_ref,
    adjf_ref,
    trans_ref,
    invm_ref,
    frac_ref,
    inter_ref,
    cols_ref,
    rows_ref,
    owner_ref,
    rankv_ref,
    ranko_ref,
    send_ref,
    recv_ref,
    hsend_ref,
    hrecv_ref,
    next_ref,
    send_sem,
    recv_sem,
    hsend_sem,
    hrecv_sem,
    next_sem,
):
    n_gx, n_gy, n_af = sizes
    tiles = n_gx * n_gy * n_af
    half = tiles // 2
    layers, width_x, width_y = press_ref.shape
    blocks, block_len = pfrac_ref.shape
    segments = blocks * block_len
    gx, gy, af = lax.axis_index("gx"), lax.axis_index("gy"), lax.axis_index("af")
    me = (gx * n_gy + gy) * n_af + af

    def place(t):
        return (t // (n_gy * n_af), (t // n_af) % n_gy, t % n_af)

    barrier = pltpu.get_barrier_semaphore()

    def greet(k, carry):
        pl.semaphore_signal(
            barrier, inc=1, device_id=place(lax.rem(me + k, tiles)), device_id_type=MESH
        )
        return carry

    lax.fori_loop(1, tiles, greet, 0)

    lane = iota((8, 128), 1)
    sub = iota((8, 128), 0)
    lane_t = iota((tiles, 128), 1)
    row_t = iota((tiles, 128), 0)
    lane_h = iota((half, 128), 1)
    left_half = lane_h < SLOT

    def flat(x):
        return jnp.concatenate([x[b : b + 1, :] for b in range(blocks)], axis=1)

    def folded(v):
        rows = [v[:, b * block_len : (b + 1) * block_len] for b in range(blocks)]
        return jnp.concatenate(rows + [jnp.zeros((8 - blocks, block_len), f32)], axis=0)

    def padded(ref):
        x = ref[...]
        return jnp.concatenate([x, jnp.zeros((8 - blocks, block_len), x.dtype)], axis=0)

    def packed_lanes(x):
        return jnp.concatenate([x[j : j + 1, :] for j in range(half)], axis=1)

    halo_to = (
        place(lax.rem(me + tiles - 1, tiles)),
        place(lax.rem(me + 1, tiles)),
        (lax.rem(gx + n_gx - 1, n_gx), gy, af),
        (lax.rem(gx + 1, n_gx), gy, af),
    )

    def halo_copy(r, side):
        return pltpu.make_async_remote_copy(
            src_ref=hsend_ref.at[r, side],
            dst_ref=hrecv_ref.at[r, side],
            send_sem=hsend_sem.at[r, side],
            recv_sem=hrecv_sem.at[r, side],
            device_id=halo_to[side],
            device_id_type=MESH,
        )

    def put_halo(r, field, extra):
        low = jnp.zeros((8, 128), f32)
        high = extra
        for z in range(layers):
            at = lane == z
            low = jnp.where(at, field[z] if z == 0 else pltpu.roll(field[z], z, 1), low)
            high = jnp.where(at, pltpu.roll(field[z], z + 1, 1), high)
        hsend_ref[r, 0] = low
        hsend_ref[r, 1] = high
        hsend_ref[r, 2] = jnp.concatenate([m[0:1, :] for m in field], axis=0)
        hsend_ref[r, 3] = jnp.concatenate([m[7:8, :] for m in field], axis=0)

    def start_halo(r):
        for side in range(4):
            halo_copy(r, side).start()

    def take_halo(r):
        for side in range(4):
            halo_copy(r, side).wait_recv()
        return [hrecv_ref[r, side] for side in range(4)]

    def neighbours(field, halo, z):
        m = field[z]
        after, before, above, below = halo
        y_up = jnp.where(lane == 127, pltpu.roll(after, 127 - z, 1), pltpu.roll(m, 127, 1))
        shifted = before if z == 0 else pltpu.roll(before, 128 - z, 1)
        y_down = jnp.where(lane == 0, shifted, pltpu.roll(m, 1, 1))
        x_up = jnp.where(sub == 7, above[z : z + 1, :], pltpu.roll(m, 7, 0))
        x_down = jnp.where(sub == 0, below[z : z + 1, :], pltpu.roll(m, 1, 0))
        return x_up, x_down, y_up, y_down

    def start_all(r):
        def one(k, carry):
            t = lax.rem(me + k, tiles)
            pltpu.make_async_remote_copy(
                src_ref=send_ref.at[r, t],
                dst_ref=recv_ref.at[r, me],
                send_sem=send_sem.at[r],
                recv_sem=recv_sem.at[r],
                device_id=place(t),
                device_id_type=MESH,
            ).start()
            return carry

        lax.fori_loop(1, tiles, one, 0)

    def wait_rows(ref, sem, r):
        part = ref.at[r, pl.ds(0, tiles - 1)]
        pltpu.make_async_copy(part, part, sem.at[r]).wait()

    def take_all(r):
        wait_rows(recv_ref, recv_sem, r)
        return jnp.where(row_t == me, send_ref[r][:, 0, :], recv_ref[r][:, 0, :])

    def put_all(r, message):
        send_ref[r] = message.reshape(tiles, 1, 128)

    def put_cross(r, field, weights):
        table = jnp.concatenate(field, axis=0)
        found = pick(table, cols_ref[...], rows_ref[...])
        first = jnp.concatenate([found[:, j * 128 : (j + 1) * 128] for j in range(half)], axis=0)
        values = jnp.concatenate([first, pltpu.roll(first, SLOT, 1)], axis=0)
        outgoing = spread(flat(weights), owner_ref[...], ranko_ref[...])
        put_all(r, jnp.where(lane_t < SLOT, values, outgoing))

    def take_cross(r):
        message = take_all(r)
        incoming = jnp.where(left_half, pltpu.roll(message[:half], SLOT, 1), message[half:])
        cells = spread(packed_lanes(incoming), rows_ref[...], cols_ref[0:128, :])
        seg_values = folded(pick(message, rankv_ref[...], owner_ref[...]))
        return [cells[8 * z : 8 * z + 8] for z in range(layers)], seg_values

    owner = flat(tile_ref[...])
    cell = flat(cell_ref[...])
    cell_row = (flat(layer_ref[...]) * width_x + cell // width_y).astype(f32)
    cell_col = (cell % width_y).astype(f32)
    owner_hot = hot(iota((tiles, segments), 0) == owner)
    owner_ref[...] = owner_hot
    groups = segments // 128
    stacked = jnp.concatenate(
        [owner_hot[:, g * 128 : (g + 1) * 128] for g in range(groups)], axis=0
    ).astype(bf16)
    tri_row = iota((128, 256), 0)
    tri_col = iota((128, 256), 1)
    counted = dot_nn(stacked, hot((tri_row < tri_col) | (tri_col >= 128)).astype(bf16))
    base = jnp.zeros((tiles, 128), f32)
    ranks = []
    for g in range(groups):
        part = counted[g * tiles : (g + 1) * tiles]
        here = owner_hot[:, g * 128 : (g + 1) * 128] * (part[:, :128] + base)
        ranks.append(jnp.sum(here, axis=0, keepdims=True))
        base = base + part[:, 128:]
    rank = jnp.concatenate(ranks, axis=1).astype(jnp.int32)
    slot = iota((128, segments), 0)
    rank_low = slot == rank
    rank_high = slot == rank + SLOT
    low_hot = hot(rank_low).astype(bf16)
    rankv_ref[0:128, :] = low_hot
    rankv_ref[128:256, :] = low_hot
    ranko_ref[...] = hot(rank_high).astype(bf16)
    asked = jnp.where(rank_low, cell_row + 1.0, jnp.where(rank_high, cell_col + 1.0, 0.0))
    put_all(0, dot_nt(owner_hot.astype(bf16), asked.astype(bf16)))

    def each_block(ref, c):
        return ref[...][:, c : c + 1]

    fsub = iota((8, block_len), 0)
    flane = iota((8, block_len), 1)
    info = jnp.zeros((8, 128), f32)
    from_hot = jnp.zeros((8, block_len), f32)
    joined_hot = []
    for c in range(blocks):
        delta, to = each_block(delta_ref, c), each_block(to_ref, c)
        info = jnp.where(
            sub == c, jnp.where(lane < 64, delta.astype(f32), to.astype(f32)), info
        )
        joined_hot.append(hot((fsub == c + delta) & (flane == to)))
        from_hot = jnp.where(
            (fsub == c) & (flane == each_block(from_ref, c)), each_block(itrans_ref, c), from_hot
        )
    cond = [cond_ref[z] for z in range(layers)]
    put_halo(0, cond, info)

    pl.semaphore_wait(barrier, tiles - 1)
    start_all(0)
    start_halo(0)
    following = pltpu.make_async_remote_copy(
        src_ref=pfrac_ref,
        dst_ref=next_ref,
        send_sem=next_sem.at[0],
        recv_sem=next_sem.at[1],
        device_id=halo_to[0],
        device_id_type=MESH,
    )
    following.start()

    position = flane
    coupling_mf, coupling_fm = padded(mf_ref), padded(fm_ref)
    press_f = padded(pfrac_ref)
    t_next = jnp.where(position < block_len - 1, padded(chain_ref), 0.0)
    t_prev = jnp.where(position > 0, pltpu.roll(t_next, 1, 1), 0.0)
    diag_f = padded(afrac_ref) + t_next + t_prev + coupling_fm
    diag_f = jnp.where(fsub < blocks, diag_f, 1.0)

    def chain(field, after, before):
        return after * pltpu.roll(field, block_len - 1, 1) + before * pltpu.roll(field, 1, 1)

    frac_ref[0] = t_next
    frac_ref[1] = t_prev
    frac_ref[2] = coupling_mf
    frac_ref[3] = coupling_fm
    frac_ref[4] = 1.0 / diag_f
    frac_ref[5] = from_hot

    well_cell = wcell_ref[...]
    wells = well_cell.shape[1]
    rate = jnp.where(wtile_ref[...] == me, wrate_ref[...], 0.0)
    well_rows = hot(iota((width_x, wells), 0) == well_cell // width_y) * rate
    well_cols = hot(iota((width_y, wells), 0) == well_cell % width_y)
    source = lax.dot_general(
        well_rows,
        well_cols,
        (((1,), (1,)), ((), ())),
        precision=lax.Precision.HIGHEST,
        preferred_element_type=f32,
    )

    asked_here = take_all(0)
    first, second = asked_here[:half], asked_here[half:]
    want_row = packed_lanes(jnp.where(left_half, first, pltpu.roll(second, SLOT, 1)))
    want_col = packed_lanes(jnp.where(left_half, pltpu.roll(first, SLOT, 1), second))
    slots = tiles * SLOT
    rows_ref[...] = hot(
        iota((layers * width_x, slots), 0) + 1 == want_row.astype(jnp.int32)
    )
    want_hot = hot(iota((width_y, slots), 0) + 1 == want_col.astype(jnp.int32)).astype(bf16)
    cols_ref[0:128, :] = want_hot
    cols_ref[128:256, :] = want_hot

    press = [press_ref[z] for z in range(layers)]
    put_halo(1, press, jnp.zeros((8, 128), f32))
    put_cross(1, press, coupling_mf * press_f)
    start_all(1)
    start_halo(1)

    halo = take_halo(0)
    along_y = gy * n_af + af
    inside_y_up = (lane < 127) | (along_y < n_gy * n_af - 1)
    inside_y_down = (lane > 0) | (along_y > 0)
    inside_x_up = (sub < 7) | (gx < n_gx - 1)
    inside_x_down = (sub > 0) | (gx > 0)
    inside = (inside_x_up, inside_x_down, inside_y_up, inside_y_down)
    diag = []
    for z in range(layers):
        total = accum_ref[z]
        near = neighbours(cond, halo, z)
        for i in range(4):
            face = jnp.where(inside[i], harmonic(cond[z], near[i]), 0.0)
            trans_ref[i, z] = face
            total = total + face
        if z + 1 < layers:
            trans_ref[4, z] = 0.5 * harmonic(cond[z], cond[z + 1])
            total = total + trans_ref[4, z]
        if z > 0:
            total = total + trans_ref[4, z - 1]
        invm_ref[z] = 1.0 / total
        diag.append(total)

    for c in range(blocks):
        inter_ref[c] = jnp.where(fsub < blocks, joined_hot[c], 0.0)
        delta = halo[1][c : c + 1, 32:33].astype(jnp.int32)
        to = halo[1][c : c + 1, 64:65].astype(jnp.int32)
        inter_ref[blocks + c] = hot(
            (fsub < blocks) & (fsub + blocks == c + delta) & (flane == to)
        )

    following.wait_recv()
    joined = jnp.concatenate([pfrac_ref[...], next_ref[...]], axis=0)
    crossing = jnp.zeros((8, block_len), f32)
    for c in range(blocks):
        found = jnp.sum(joined_hot[c] * joined, axis=1, keepdims=True)
        found = jnp.sum(found, axis=0, keepdims=True)
        crossing = jnp.where(fsub == c, from_hot * found, crossing)

    def stencil(field, halo, z):
        near = neighbours(field, halo, z)
        total = trans_ref[0, z] * near[0]
        for i in range(1, 4):
            total = total + trans_ref[i, z] * near[i]
        if z + 1 < layers:
            total = total + trans_ref[4, z] * field[z + 1]
        if z > 0:
            total = total + trans_ref[4, z - 1] * field[z - 1]
        return total

    halo = take_halo(1)
    around = [stencil(press, halo, z) for z in range(layers)]
    cells, seg_values = take_cross(1)
    for z in range(layers):
        res = diag[z] * press[z] - around[z] - cells[z] - source
        resm_ref[z] = res
        adjm_ref[z] = res * invm_ref[z]
    res_f = diag_f * press_f - chain(press_f, t_next, t_prev) - coupling_fm * seg_values - crossing
    resf_ref[...] = res_f[:blocks]
    adjf_ref[...] = (res_f * frac_ref[4])[:blocks]

    def sweep(r, carry):
        field = [adjm_ref[z] for z in range(layers)]
        frac = padded(adjf_ref)
        sent = jnp.sum(frac_ref[5] * frac, axis=1, keepdims=True)
        put_halo(r, field, jnp.broadcast_to(sent, (8, 128)))
        start_halo(r)
        put_cross(r, field, frac_ref[3] * frac)
        start_all(r)
        total = padded(resf_ref) + chain(frac, frac_ref[0], frac_ref[1])
        for c in range(blocks):
            total = total + inter_ref[c] * sent[c : c + 1, :]
        halo = take_halo(r)
        around = [stencil(field, halo, z) for z in range(layers)]
        for c in range(blocks):
            total = total + inter_ref[blocks + c] * halo[1][c : c + 1, 64:65]
        cells, seg_values = take_cross(r)
        for z in range(layers):
            adjm_ref[z] = (resm_ref[z] + around[z] + cells[z]) * invm_ref[z]
        total = total + frac_ref[2] * seg_values
        adjf_ref[...] = (total * frac_ref[4])[:blocks]
        return carry

    lax.fori_loop(2, ROUNDS, sweep, 0)

    following.wait_send()

    def finish(r, carry):
        wait_rows(send_ref, send_sem, r)
        for side in range(4):
            halo_copy(r, side).wait_send()
        return carry

    lax.fori_loop(0, ROUNDS, finish, 0)


def body(sizes, *args):
    press_matrix, press_frac = args[0], args[3]
    args = list(args)
    for i in range(11, 18):
        args[i] = args[i].reshape(1, -1)
    tiles = sizes[0] * sizes[1] * sizes[2]
    layers, width_x, width_y = press_matrix.shape
    blocks, block_len = press_frac.shape
    segments = blocks * block_len
    slots = tiles * SLOT
    vmem = pl.BlockSpec(memory_space=pltpu.VMEM)
    matrix = jax.ShapeDtypeStruct(press_matrix.shape, f32)
    fracture = jax.ShapeDtypeStruct(press_frac.shape, f32)
    return pl.pallas_call(
        functools.partial(kernel, sizes),
        out_shape=(matrix, fracture, matrix, fracture),
        in_specs=[vmem] * 18,
        out_specs=(vmem,) * 4,
        scratch_shapes=[
            pltpu.VMEM((5, layers, width_x, width_y), f32),
            pltpu.VMEM((layers, width_x, width_y), f32),
            pltpu.VMEM((6, 8, block_len), f32),
            pltpu.VMEM((2 * blocks, 8, block_len), f32),
            pltpu.VMEM((2 * width_y, slots), bf16),
            pltpu.VMEM((layers * width_x, slots), f32),
            pltpu.VMEM((tiles, segments), f32),
            pltpu.VMEM((256, segments), bf16),
            pltpu.VMEM((128, segments), bf16),
            pltpu.VMEM((ROUNDS, tiles, 1, 128), f32),
            pltpu.VMEM((ROUNDS, tiles, 1, 128), f32),
            pltpu.VMEM((ROUNDS, 4, 8, 128), f32),
            pltpu.VMEM((ROUNDS, 4, 8, 128), f32),
            pltpu.VMEM((blocks, block_len), f32),
            pltpu.SemaphoreType.DMA((ROUNDS,)),
            pltpu.SemaphoreType.DMA((ROUNDS,)),
            pltpu.SemaphoreType.DMA((ROUNDS, 4)),
            pltpu.SemaphoreType.DMA((ROUNDS, 4)),
            pltpu.SemaphoreType.DMA((2,)),
        ],
        compiler_params=pltpu.CompilerParams(
            collective_id=0, has_side_effects=True, vmem_limit_bytes=40 * 1024 * 1024
        ),
    )(*args)


def solution(mesh):
    slab = P(None, "gx", ("gy", "af"))
    fracture = P(("gx", "gy", "af"), None)
    block = P(("gx", "gy", "af"))
    in_specs = (slab,) * 3 + (fracture,) * 8 + (block,) * 4 + (P(),) * 3
    out_specs = (slab, fracture, slab, fracture)
    sizes = tuple(mesh.shape[axis] for axis in ("gx", "gy", "af"))
    return jax.shard_map(
        functools.partial(body, sizes),
        mesh=mesh,
        in_specs=in_specs,
        out_specs=out_specs,
        check_vma=False,
    )
```

```python
import functools

import jax
import jax.numpy as jnp
from jax import lax
from jax.experimental import pallas as pl
from jax.experimental.pallas import tpu as pltpu
from jax.sharding import PartitionSpec as P

ITERS = 8
ROUNDS = ITERS + 1
SLOT = 64
LOGICAL = pl.DeviceIdType.LOGICAL
f32 = jnp.float32
bf16 = jnp.bfloat16


def harmonic(first, second):
    return 2.0 * first * second / (first + second)


def iota(shape, dim):
    return lax.broadcasted_iota(jnp.int32, shape, dim)


def hot(mask):
    return jnp.where(mask, 1.0, 0.0)


def pieces(values):
    high = values.astype(bf16)
    return high, (values - high.astype(f32)).astype(bf16)


def dot_nn(a, b):
    return lax.dot_general(a, b, (((1,), (0,)), ((), ())), preferred_element_type=f32)


def dot_nt(a, b):
    return lax.dot_general(a, b, (((1,), (1,)), ((), ())), preferred_element_type=f32)


def taken(row, lanes):
    return jnp.take_along_axis(
        jnp.broadcast_to(row, lanes.shape), lanes, axis=1, mode="promise_in_bounds"
    )


def by_eight(x):
    return [x[8 * q : 8 * q + 8] for q in range(x.shape[0] // 8)]


def kernel(sizes, *refs):
    hbm, outs, held, rest = refs[:18], refs[18:22], refs[22:40], refs[40:]
    resm_ref, resf_ref, adjm_ref, adjf_ref = outs
    (
        trans_ref,
        invm_ref,
        frac_ref,
        inter_ref,
        cols_ref,
        rows_ref,
        index_ref,
        slot_ref,
        seg_ref,
        send_ref,
        recv_ref,
        hsend_ref,
        hrecv_ref,
        next_ref,
        load_sem,
        send_sem,
        recv_sem,
        hsend_sem,
        hrecv_sem,
        next_sem,
    ) = rest
    n_gx, n_gy, n_af = sizes
    tiles = n_gx * n_gy * n_af
    half = tiles // 2
    gx, gy, af = lax.axis_index("gx"), lax.axis_index("gy"), lax.axis_index("af")
    me = (gx * n_gy + gy) * n_af + af
    barrier = pltpu.get_barrier_semaphore()

    loads = [pltpu.make_async_copy(hbm[i], held[i], load_sem.at[i]) for i in range(18)]
    for i in (8, 9, 10, 1, 11, 13, 3, 12, 14, 0, 4, 5, 6, 7, 15, 16, 17, 2):
        loads[i].start()

    def wrapped(k):
        return lax.rem(me + k, tiles)

    for k in range(1, tiles):
        pl.semaphore_signal(
            barrier, inc=1, device_id=wrapped(k), device_id_type=LOGICAL
        )

    def loaded(i):
        loads[i].wait()
        return held[i]

    press_ref, cond_ref = held[0], held[1]
    layers, width_x, width_y = press_ref.shape
    blocks, block_len = held[3].shape

    lane = iota((8, 128), 1)
    sub = iota((8, 128), 0)
    block_of = sub % blocks
    position = lane + 128 * (sub // blocks)
    row_t = iota((tiles, 128), 0)
    lane_t = iota((tiles, 128), 1)
    left_half = iota((half, 128), 1) < SLOT

    def folded(x):
        return jnp.concatenate([x[:, :128], x[:, 128:]], axis=0)

    def unfolded(x):
        return jnp.concatenate([x[:blocks], x[blocks:]], axis=1)

    halo_to = (
        wrapped(tiles - 1),
        wrapped(1),
        wrapped(tiles - n_gy * n_af),
        wrapped(n_gy * n_af),
    )

    def halo_copy(r, side):
        return pltpu.make_async_remote_copy(
            src_ref=hsend_ref.at[r, side],
            dst_ref=hrecv_ref.at[r, side],
            send_sem=hsend_sem.at[r, side],
            recv_sem=hrecv_sem.at[r, side],
            device_id=halo_to[side],
            device_id_type=LOGICAL,
        )

    def put_halo(r, field, extra):
        low = jnp.zeros((8, 128), f32)
        high = extra
        for z in range(layers):
            at = lane == z
            low = jnp.where(at, field[z] if z == 0 else pltpu.roll(field[z], z, 1), low)
            high = jnp.where(at, pltpu.roll(field[z], z + 1, 1), high)
        hsend_ref[r, 0] = low
        hsend_ref[r, 1] = high
        hsend_ref[r, 2] = jnp.concatenate([m[0:1, :] for m in field], axis=0)
        hsend_ref[r, 3] = jnp.concatenate([m[7:8, :] for m in field], axis=0)

    def start_halo(r):
        for side in range(4):
            halo_copy(r, side).start()

    def take_halo(r):
        for side in range(4):
            halo_copy(r, side).wait_recv()
        return [hrecv_ref[r, side] for side in range(4)]

    def neighbours(field, halo, z):
        m = field[z]
        after, before, above, below = halo
        y_up = jnp.where(lane == 127, pltpu.roll(after, 127 - z, 1), pltpu.roll(m, 127, 1))
        shifted = before if z == 0 else pltpu.roll(before, 128 - z, 1)
        y_down = jnp.where(lane == 0, shifted, pltpu.roll(m, 1, 1))
        x_up = jnp.where(sub == 7, above[z : z + 1, :], pltpu.roll(m, 7, 0))
        x_down = jnp.where(sub == 0, below[z : z + 1, :], pltpu.roll(m, 1, 0))
        return x_up, x_down, y_up, y_down

    def start_all(r):
        for k in range(1, tiles):
            t = wrapped(k)
            pltpu.make_async_remote_copy(
                src_ref=send_ref.at[r, t],
                dst_ref=recv_ref.at[r, me],
                send_sem=send_sem.at[r],
                recv_sem=recv_sem.at[r],
                device_id=t,
                device_id_type=LOGICAL,
            ).start()

    def wait_rows(ref, sem, r):
        part = ref.at[r, pl.ds(0, tiles - 1)]
        pltpu.make_async_copy(part, part, sem.at[r]).wait()

    def put_all(r, message):
        send_ref[r] = message.reshape(tiles, 1, 128)
        recv_ref[r, me] = send_ref[r, me]

    def take_all(r):
        wait_rows(recv_ref, recv_sem, r)
        return recv_ref[r][:, 0, :]

    def put_cross(r, field_ref, weights):
        wanted = []
        for q in range(half // 8):
            at_row = index_ref[0, 8 * q : 8 * q + 8]
            at_lane = index_ref[1, 8 * q : 8 * q + 8]
            found = jnp.zeros((8, 128), f32)
            for z in range(layers):
                for x in range(width_x):
                    got = taken(field_ref[z, x : x + 1, :], at_lane)
                    found = jnp.where(at_row == z * width_x + x, got, found)
            wanted.append(found)
        values = wanted + [pltpu.roll(v, SLOT, 1) for v in wanted]
        rows = [jnp.broadcast_to(weights[i : i + 1, :], (8, 128)) for i in range(8)]
        message = []
        for q in range(tiles // 8):
            at_row = slot_ref[0, 8 * q : 8 * q + 8]
            at_lane = slot_ref[1, 8 * q : 8 * q + 8]
            found = jnp.zeros((8, 128), f32)
            for i in range(8):
                found = jnp.where(at_row == i, taken(rows[i], at_lane), found)
            message.append(jnp.where(lane < SLOT, values[q], found))
        put_all(r, jnp.concatenate(message, axis=0))

    def take_cross(r):
        message = take_all(r)
        incoming = jnp.where(left_half, pltpu.roll(message[:half], SLOT, 1), message[half:])
        high, low = pieces(incoming)
        parts = []
        for piece in (high.astype(f32), low.astype(f32)):
            scaled = []
            for j in range(half):
                one = jnp.broadcast_to(piece[j : j + 1, :], (16, 128)).astype(bf16)
                wide = jnp.concatenate([one] * (layers * width_x // 16), axis=0)
                scaled.append(rows_ref[:, 128 * j : 128 * j + 128] * wide)
            parts.append(jnp.concatenate(scaled, axis=1))
        both = dot_nt(jnp.concatenate(parts, axis=0), cols_ref[...])
        cells = both[: layers * width_x] + both[layers * width_x :]
        of, rank = seg_ref[0], seg_ref[1]
        seg_values = jnp.zeros((8, 128), f32)
        for t in range(tiles):
            seg_values = jnp.where(of == t, taken(recv_ref[r, t], rank), seg_values)
        return [cells[8 * z : 8 * z + 8] for z in range(layers)], seg_values

    owner = folded(loaded(8)[...])
    layer = folded(loaded(9)[...])
    cell = folded(loaded(10)[...])
    cell_row = (layer * width_x + cell // width_y).astype(f32) + 1.0
    cell_col = (cell % width_y).astype(f32) + 1.0
    owner_hot = [hot(row_t == owner[g : g + 1, :]) for g in range(8)]
    tri_row = iota((128, 256), 0)
    tri_col = iota((128, 256), 1)
    counted = dot_nn(
        jnp.concatenate(owner_hot, axis=0).astype(bf16),
        hot((tri_row < tri_col) | (tri_col >= 128)).astype(bf16),
    )
    base = jnp.zeros((tiles, 128), f32)
    ranks = []
    for g in range(8):
        part = counted[g * tiles : (g + 1) * tiles]
        ranks.append(jnp.sum(owner_hot[g] * (part[:, :128] + base), axis=0, keepdims=True))
        base = base + part[:, 128:]
    rank = jnp.concatenate(ranks, axis=0).astype(jnp.int32)
    seg_ref[0] = owner
    seg_ref[1] = rank
    slot = iota((128, 128), 0)
    lane_up = iota((128, 128), 1).astype(f32) + 1.0
    asked, origin = [], []
    for g in range(8):
        low = slot == rank[g : g + 1, :]
        high = slot == rank[g : g + 1, :] + SLOT
        asked.append(
            jnp.where(low, cell_row[g : g + 1, :], jnp.where(high, cell_col[g : g + 1, :], 0.0))
        )
        origin.append(jnp.where(low, lane_up, jnp.where(high, g + 1.0, 0.0)))
    table = jnp.concatenate(
        [jnp.concatenate(asked, axis=1), jnp.concatenate(origin, axis=1)], axis=0
    )
    spread = dot_nt(jnp.concatenate(owner_hot, axis=1).astype(bf16), table.astype(bf16))
    put_all(0, spread[:, :128])
    origin = spread[:, 128:]
    origin_row = jnp.where(lane_t < SLOT, 0.0, origin)
    slot_ref[0] = origin_row.astype(jnp.int32) - 1
    slot_ref[1] = jnp.maximum(pltpu.roll(origin, SLOT, 1).astype(jnp.int32) - 1, 0)

    cond_ref = loaded(1)
    cond = [cond_ref[z] for z in range(layers)]
    all_delta, all_to = loaded(11)[...], loaded(13)[...]
    info = jnp.zeros((8, 128), f32)
    near_hot, next_hot = [], []
    for c in range(blocks):
        delta, to = all_delta[:, c : c + 1], all_to[:, c : c + 1]
        info = jnp.where(
            sub == c, jnp.where(lane < 64, delta.astype(f32), to.astype(f32)), info
        )
        near_hot.append(hot((block_of == c + delta) & (position == to)))
        next_hot.append(hot((block_of + blocks == c + delta) & (position == to)))
        inter_ref[c] = near_hot[c]
    put_halo(0, cond, info)
    pfrac_ref = loaded(3)

    pl.semaphore_wait(barrier, tiles - 1)
    start_all(0)
    start_halo(0)
    following = pltpu.make_async_remote_copy(
        src_ref=pfrac_ref,
        dst_ref=next_ref,
        send_sem=next_sem.at[0],
        recv_sem=next_sem.at[1],
        device_id=halo_to[0],
        device_id_type=LOGICAL,
    )
    following.start()

    all_from, all_trans = loaded(12)[...], loaded(14)[...]
    from_hot = jnp.zeros((8, 128), f32)
    for c in range(blocks):
        from_hot = jnp.where(
            (block_of == c) & (position == all_from[:, c : c + 1]),
            all_trans[:, c : c + 1],
            from_hot,
        )

    def later(x):
        moved = pltpu.roll(x, 127, 1)
        return jnp.where(lane == 127, pltpu.roll(moved, blocks, 0), moved)

    def earlier(x):
        moved = pltpu.roll(x, 1, 1)
        return jnp.where(lane == 0, pltpu.roll(moved, blocks, 0), moved)

    def chain(field, after, before):
        return after * later(field) + before * earlier(field)

    loaded(0)
    press = [press_ref[z] for z in range(layers)]
    press_f = folded(pfrac_ref[...])
    accum_f = folded(loaded(4)[...])
    t_next = jnp.where(position < block_len - 1, folded(loaded(5)[...]), 0.0)
    t_prev = jnp.where(position > 0, earlier(t_next), 0.0)
    coupling_mf = folded(loaded(6)[...])
    coupling_fm = folded(loaded(7)[...])
    diag_f = accum_f + t_next + t_prev + coupling_fm
    frac_ref[0] = t_next
    frac_ref[1] = t_prev
    frac_ref[2] = coupling_mf
    frac_ref[3] = coupling_fm
    frac_ref[4] = 1.0 / diag_f
    frac_ref[5] = from_hot

    well_tile, well_cell, well_rate = loaded(15)[...], loaded(16)[...], loaded(17)[...]
    wells = well_cell.shape[1]
    rate = jnp.where(well_tile == me, well_rate, 0.0)
    source = lax.dot_general(
        hot(iota((width_x, wells), 0) == well_cell // width_y) * rate,
        hot(iota((width_y, wells), 0) == well_cell % width_y),
        (((1,), (1,)), ((), ())),
        precision=lax.Precision.HIGHEST,
        preferred_element_type=f32,
    )
    accum_ref = loaded(2)
    put_halo(1, press, jnp.zeros((8, 128), f32))
    start_halo(1)

    halo = take_halo(0)
    along_y = gy * n_af + af
    inside = (
        (sub < 7) | (gx < n_gx - 1),
        (sub > 0) | (gx > 0),
        (lane < 127) | (along_y < n_gy * n_af - 1),
        (lane > 0) | (along_y > 0),
    )
    diag = []
    for z in range(layers):
        total = accum_ref[z]
        near = neighbours(cond, halo, z)
        for i in range(4):
            face = jnp.where(inside[i], harmonic(cond[z], near[i]), 0.0)
            trans_ref[i, z] = face
            total = total + face
        if z + 1 < layers:
            trans_ref[4, z] = 0.5 * harmonic(cond[z], cond[z + 1])
            total = total + trans_ref[4, z]
        if z > 0:
            total = total + trans_ref[4, z - 1]
        invm_ref[z] = 1.0 / total
        diag.append(total)
    for c in range(blocks):
        delta = halo[1][c : c + 1, 32:33].astype(jnp.int32)
        to = halo[1][c : c + 1, 64:65].astype(jnp.int32)
        inter_ref[blocks + c] = hot((block_of + blocks == c + delta) & (position == to))

    asked_here = take_all(0)
    first, second = asked_here[:half], asked_here[half:]
    want_row = jnp.where(left_half, first, pltpu.roll(second, SLOT, 1)).astype(jnp.int32) - 1
    want_col = jnp.where(left_half, pltpu.roll(first, SLOT, 1), second).astype(jnp.int32) - 1
    index_ref[0] = want_row
    index_ref[1] = jnp.maximum(want_col, 0)

    put_cross(1, press_ref, coupling_mf * press_f)
    start_all(1)
    for j in range(half):
        at = slice(128 * j, 128 * j + 128)
        rows_ref[:, at] = hot(
            iota((layers * width_x, 128), 0) == want_row[j : j + 1, :]
        ).astype(bf16)
        cols_ref[:, at] = hot(iota((width_y, 128), 0) == want_col[j : j + 1, :]).astype(bf16)

    following.wait_recv()
    next_f = folded(next_ref[...])
    crossing = jnp.zeros((8, 128), f32)
    for c in range(blocks):
        found = jnp.sum(near_hot[c] * press_f + next_hot[c] * next_f, axis=1, keepdims=True)
        found = jnp.sum(found, axis=0, keepdims=True)
        crossing = jnp.where(block_of == c, from_hot * found, crossing)

    def stencil(field, halo, z):
        near = neighbours(field, halo, z)
        total = trans_ref[0, z] * near[0]
        for i in range(1, 4):
            total = total + trans_ref[i, z] * near[i]
        if z + 1 < layers:
            total = total + trans_ref[4, z] * field[z + 1]
        if z > 0:
            total = total + trans_ref[4, z - 1] * field[z - 1]
        return total

    halo = take_halo(1)
    around = [stencil(press, halo, z) for z in range(layers)]
    cells, seg_values = take_cross(1)
    for z in range(layers):
        res = diag[z] * press[z] - around[z] - cells[z] - source
        resm_ref[z] = res
        adjm_ref[z] = res * invm_ref[z]
    res_f = diag_f * press_f - chain(press_f, t_next, t_prev) - coupling_fm * seg_values - crossing
    resf_ref[...] = unfolded(res_f)
    frac_ref[6] = res_f
    frac_ref[7] = res_f * frac_ref[4]

    def sweep(r, carry):
        field = [adjm_ref[z] for z in range(layers)]
        frac = frac_ref[7]
        sent = jnp.sum(frac_ref[5] * frac, axis=1, keepdims=True)
        sent = sent[:blocks] + sent[blocks:]
        put_halo(r, field, jnp.broadcast_to(jnp.concatenate([sent, sent], axis=0), (8, 128)))
        start_halo(r)
        put_cross(r, adjm_ref, frac_ref[3] * frac)
        start_all(r)
        total = frac_ref[6] + chain(frac, frac_ref[0], frac_ref[1])
        for c in range(blocks):
            total = total + inter_ref[c] * sent[c : c + 1, :]
        halo = take_halo(r)
        around = [resm_ref[z] + stencil(field, halo, z) for z in range(layers)]
        for c in range(blocks):
            total = total + inter_ref[blocks + c] * halo[1][c : c + 1, 64:65]
        cells, seg_values = take_cross(r)
        for z in range(layers):
            adjm_ref[z] = (around[z] + cells[z]) * invm_ref[z]
        frac_ref[7] = (total + frac_ref[2] * seg_values) * frac_ref[4]
        return carry

    lax.fori_loop(2, ROUNDS, sweep, 0)
    adjf_ref[...] = unfolded(frac_ref[7])

    following.wait_send()

    def finish(r, carry):
        wait_rows(send_ref, send_sem, r)
        for side in range(4):
            halo_copy(r, side).wait_send()
        return carry

    lax.fori_loop(0, ROUNDS, finish, 0)


def copy_out(*refs):
    sems = refs[8]
    copies = [pltpu.make_async_copy(refs[i], refs[4 + i], sems.at[i]) for i in range(4)]
    for copy in copies:
        copy.start()
    for copy in copies:
        copy.wait()


def body(sizes, *args):
    press_matrix, press_frac = args[0], args[3]
    args = list(args)
    for i in range(11, 18):
        args[i] = args[i].reshape(1, -1)
    tiles = sizes[0] * sizes[1] * sizes[2]
    layers, width_x, width_y = press_matrix.shape
    blocks, block_len = press_frac.shape
    slots = tiles * SLOT
    vmem = pl.BlockSpec(memory_space=pltpu.VMEM)
    anywhere = pl.BlockSpec(memory_space=pl.ANY)
    matrix = jax.ShapeDtypeStruct(press_matrix.shape, f32)
    fracture = jax.ShapeDtypeStruct(press_frac.shape, f32)
    out_shape = (matrix, fracture, matrix, fracture)
    results = pl.pallas_call(
        functools.partial(kernel, sizes),
        out_shape=out_shape,
        in_specs=[anywhere] * 18,
        out_specs=(vmem,) * 4,
        scratch_shapes=[pltpu.VMEM(x.shape, x.dtype) for x in args]
        + [
            pltpu.VMEM((5, layers, width_x, width_y), f32),
            pltpu.VMEM((layers, width_x, width_y), f32),
            pltpu.VMEM((8, 8, 128), f32),
            pltpu.VMEM((2 * blocks, 8, 128), f32),
            pltpu.VMEM((width_y, slots), bf16),
            pltpu.VMEM((layers * width_x, slots), bf16),
            pltpu.VMEM((2, tiles // 2, 128), jnp.int32),
            pltpu.VMEM((2, tiles, 128), jnp.int32),
            pltpu.VMEM((2, 8, 128), jnp.int32),
            pltpu.VMEM((ROUNDS, tiles, 1, 128), f32),
            pltpu.VMEM((ROUNDS, tiles, 1, 128), f32),
            pltpu.VMEM((ROUNDS, 4, 8, 128), f32),
            pltpu.VMEM((ROUNDS, 4, 8, 128), f32),
            pltpu.VMEM((blocks, block_len), f32),
            pltpu.SemaphoreType.DMA((18,)),
            pltpu.SemaphoreType.DMA((ROUNDS,)),
            pltpu.SemaphoreType.DMA((ROUNDS,)),
            pltpu.SemaphoreType.DMA((ROUNDS, 4)),
            pltpu.SemaphoreType.DMA((ROUNDS, 4)),
            pltpu.SemaphoreType.DMA((2,)),
        ],
        compiler_params=pltpu.CompilerParams(
            collective_id=0, has_side_effects=True, vmem_limit_bytes=60 * 1024 * 1024
        ),
    )(*args)
    return pl.pallas_call(
        copy_out,
        out_shape=out_shape,
        in_specs=[anywhere] * 4,
        out_specs=(anywhere,) * 4,
        scratch_shapes=[pltpu.SemaphoreType.DMA((4,))],
        compiler_params=pltpu.CompilerParams(vmem_limit_bytes=60 * 1024 * 1024),
    )(*results)


def solution(mesh):
    slab = P(None, "gx", ("gy", "af"))
    fracture = P(("gx", "gy", "af"), None)
    block = P(("gx", "gy", "af"))
    in_specs = (slab,) * 3 + (fracture,) * 8 + (block,) * 4 + (P(),) * 3
    out_specs = (slab, fracture, slab, fracture)
    sizes = tuple(mesh.shape[axis] for axis in ("gx", "gy", "af"))
    return jax.shard_map(
        functools.partial(body, sizes),
        mesh=mesh,
        in_specs=in_specs,
        out_specs=out_specs,
        check_vma=False,
    )
```

```python
import functools

import jax
import jax.numpy as jnp
from jax import lax
from jax.experimental import pallas as pl
from jax.experimental.pallas import tpu as pltpu
from jax.sharding import PartitionSpec as P

ITERS = 8
ROUNDS = ITERS + 1
SLOT = 64
LOGICAL = pl.DeviceIdType.LOGICAL
f32 = jnp.float32
bf16 = jnp.bfloat16


def harmonic(first, second):
    return 2.0 * first * second / (first + second)


def iota(shape, dim):
    return lax.broadcasted_iota(jnp.int32, shape, dim)


def hot(mask):
    return jnp.where(mask, 1.0, 0.0)


def pieces(values):
    high = values.astype(bf16)
    return high, (values - high.astype(f32)).astype(bf16)


def dot_nn(a, b):
    return lax.dot_general(a, b, (((1,), (0,)), ((), ())), preferred_element_type=f32)


def dot_nt(a, b):
    return lax.dot_general(a, b, (((1,), (1,)), ((), ())), preferred_element_type=f32)


def taken(row, lanes):
    return jnp.take_along_axis(
        jnp.broadcast_to(row, lanes.shape), lanes, axis=1, mode="promise_in_bounds"
    )


def by_eight(x):
    return [x[8 * q : 8 * q + 8] for q in range(x.shape[0] // 8)]


def kernel(sizes, *refs):
    hbm, outs, held, rest = refs[:18], refs[18:22], refs[22:40], refs[40:]
    resm_ref, resf_ref, adjm_ref, adjf_ref = outs
    (
        trans_ref,
        invm_ref,
        frac_ref,
        inter_ref,
        cols_ref,
        rows_ref,
        index_ref,
        slot_ref,
        seg_ref,
        send_ref,
        recv_ref,
        hsend_ref,
        hrecv_ref,
        next_ref,
        load_sem,
        send_sem,
        recv_sem,
        hsend_sem,
        hrecv_sem,
        next_sem,
    ) = rest
    n_gx, n_gy, n_af = sizes
    tiles = n_gx * n_gy * n_af
    half = tiles // 2
    gx, gy, af = lax.axis_index("gx"), lax.axis_index("gy"), lax.axis_index("af")
    me = (gx * n_gy + gy) * n_af + af
    barrier = pltpu.get_barrier_semaphore()

    loads = [pltpu.make_async_copy(hbm[i], held[i], load_sem.at[i]) for i in range(18)]
    for i in (8, 9, 10, 1, 11, 13, 3, 12, 14, 0, 4, 5, 6, 7, 15, 16, 17, 2):
        loads[i].start()

    def wrapped(k):
        return lax.rem(me + k, tiles)

    for k in range(1, tiles):
        pl.semaphore_signal(
            barrier, inc=1, device_id=wrapped(k), device_id_type=LOGICAL
        )

    def loaded(i):
        loads[i].wait()
        return held[i]

    press_ref, cond_ref = held[0], held[1]
    layers, width_x, width_y = press_ref.shape
    blocks, block_len = held[3].shape

    lane = iota((8, 128), 1)
    sub = iota((8, 128), 0)
    block_of = sub % blocks
    position = lane + 128 * (sub // blocks)
    row_t = iota((tiles, 128), 0)
    lane_t = iota((tiles, 128), 1)
    left_half = iota((half, 128), 1) < SLOT

    def folded(x):
        return jnp.concatenate([x[:, :128], x[:, 128:]], axis=0)

    def unfolded(x):
        return jnp.concatenate([x[:blocks], x[blocks:]], axis=1)

    halo_to = (
        wrapped(tiles - 1),
        wrapped(1),
        wrapped(tiles - n_gy * n_af),
        wrapped(n_gy * n_af),
    )

    def halo_copy(r, side):
        return pltpu.make_async_remote_copy(
            src_ref=hsend_ref.at[r, side],
            dst_ref=hrecv_ref.at[r, side],
            send_sem=hsend_sem.at[r, side],
            recv_sem=hrecv_sem.at[r, side],
            device_id=halo_to[side],
            device_id_type=LOGICAL,
        )

    def put_halo(r, field, extra):
        low = jnp.zeros((8, 128), f32)
        high = extra
        for z in range(layers):
            at = lane == z
            low = jnp.where(at, field[z] if z == 0 else pltpu.roll(field[z], z, 1), low)
            high = jnp.where(at, pltpu.roll(field[z], z + 1, 1), high)
        hsend_ref[r, 0] = low
        hsend_ref[r, 1] = high
        hsend_ref[r, 2] = jnp.concatenate([m[0:1, :] for m in field], axis=0)
        hsend_ref[r, 3] = jnp.concatenate([m[7:8, :] for m in field], axis=0)

    def start_halo(r):
        for side in range(4):
            halo_copy(r, side).start()

    def take_halo(r):
        for side in range(4):
            halo_copy(r, side).wait_recv()
        return [hrecv_ref[r, side] for side in range(4)]

    def neighbours(field, halo, z):
        m = field[z]
        after, before, above, below = halo
        y_up = jnp.where(lane == 127, pltpu.roll(after, 127 - z, 1), pltpu.roll(m, 127, 1))
        shifted = before if z == 0 else pltpu.roll(before, 128 - z, 1)
        y_down = jnp.where(lane == 0, shifted, pltpu.roll(m, 1, 1))
        x_up = jnp.where(sub == 7, above[z : z + 1, :], pltpu.roll(m, 7, 0))
        x_down = jnp.where(sub == 0, below[z : z + 1, :], pltpu.roll(m, 1, 0))
        return x_up, x_down, y_up, y_down

    def put_eight(r, q, message):
        send_ref[r, 8 * q : 8 * q + 8] = message.reshape(8, 1, 128)
        if q == 0:
            recv_ref[r, 0] = message[0:1, :]
        for k in range(max(8 * q, 1), 8 * q + 8):
            pltpu.make_async_remote_copy(
                src_ref=send_ref.at[r, k],
                dst_ref=recv_ref.at[r, tiles - k],
                send_sem=send_sem.at[r],
                recv_sem=recv_sem.at[r],
                device_id=wrapped(k),
                device_id_type=LOGICAL,
            ).start()

    def wait_rows(ref, sem, r):
        part = ref.at[r, pl.ds(0, tiles - 1)]
        pltpu.make_async_copy(part, part, sem.at[r]).wait()

    def take_all(r):
        wait_rows(recv_ref, recv_sem, r)
        return recv_ref[r][:, 0, :]

    def put_cross(r, field_ref, weights):
        rows = [jnp.broadcast_to(weights[i : i + 1, :], (8, 128)) for i in range(8)]
        for q in range(half // 8):
            at_row = index_ref[0, 8 * q : 8 * q + 8]
            at_lane = index_ref[1, 8 * q : 8 * q + 8]
            wanted = jnp.zeros((8, 128), f32)
            for z in range(layers):
                for x in range(width_x):
                    got = taken(field_ref[z, x : x + 1, :], at_lane)
                    wanted = jnp.where(at_row == z * width_x + x, got, wanted)
            for p, values in ((q + half // 8, pltpu.roll(wanted, SLOT, 1)), (q, wanted)):
                at_row = slot_ref[0, 8 * p : 8 * p + 8]
                at_lane = slot_ref[1, 8 * p : 8 * p + 8]
                found = jnp.zeros((8, 128), f32)
                for i in range(8):
                    found = jnp.where(at_row == i, taken(rows[i], at_lane), found)
                put_eight(r, p, jnp.where(lane < SLOT, values, found))

    def take_cross(r):
        message = take_all(r)
        incoming = jnp.where(left_half, pltpu.roll(message[:half], SLOT, 1), message[half:])
        high, low = pieces(incoming)
        parts = []
        for piece in (high.astype(f32), low.astype(f32)):
            scaled = []
            for j in range(half):
                one = jnp.broadcast_to(piece[j : j + 1, :], (16, 128)).astype(bf16)
                wide = jnp.concatenate([one] * (layers * width_x // 16), axis=0)
                scaled.append(rows_ref[:, 128 * j : 128 * j + 128] * wide)
            parts.append(jnp.concatenate(scaled, axis=1))
        both = dot_nt(jnp.concatenate(parts, axis=0), cols_ref[...])
        cells = both[: layers * width_x] + both[layers * width_x :]
        of, rank = seg_ref[0], seg_ref[1]
        seg_values = jnp.zeros((8, 128), f32)
        for t in range(tiles):
            seg_values = jnp.where(of == t, taken(recv_ref[r, t], rank), seg_values)
        return [cells[8 * z : 8 * z + 8] for z in range(layers)], seg_values

    owner = folded(loaded(8)[...]) - me
    owner = jnp.where(owner < 0, owner + tiles, owner)
    layer = folded(loaded(9)[...])
    cell = folded(loaded(10)[...])
    cell_row = (layer * width_x + cell // width_y).astype(f32) + 1.0
    cell_col = (cell % width_y).astype(f32) + 1.0
    owner_hot = [hot(row_t == owner[g : g + 1, :]) for g in range(8)]
    tri_row = iota((128, 256), 0)
    tri_col = iota((128, 256), 1)
    counted = dot_nn(
        jnp.concatenate(owner_hot, axis=0).astype(bf16),
        hot((tri_row < tri_col) | (tri_col >= 128)).astype(bf16),
    )
    base = jnp.zeros((tiles, 128), f32)
    ranks = []
    for g in range(8):
        part = counted[g * tiles : (g + 1) * tiles]
        ranks.append(jnp.sum(owner_hot[g] * (part[:, :128] + base), axis=0, keepdims=True))
        base = base + part[:, 128:]
    rank = jnp.concatenate(ranks, axis=0).astype(jnp.int32)
    seg_ref[0] = owner
    seg_ref[1] = rank
    slot = iota((128, 128), 0)
    lane_up = iota((128, 128), 1).astype(f32) + 1.0
    asked, origin = [], []
    for g in range(8):
        low = slot == rank[g : g + 1, :]
        high = slot == rank[g : g + 1, :] + SLOT
        asked.append(
            jnp.where(low, cell_row[g : g + 1, :], jnp.where(high, cell_col[g : g + 1, :], 0.0))
        )
        origin.append(jnp.where(low, lane_up, jnp.where(high, g + 1.0, 0.0)))
    table = jnp.concatenate(
        [jnp.concatenate(asked, axis=1), jnp.concatenate(origin, axis=1)], axis=0
    )
    spread = dot_nt(jnp.concatenate(owner_hot, axis=1).astype(bf16), table.astype(bf16))
    requests = spread[:, :128]
    origin = spread[:, 128:]
    origin_row = jnp.where(lane_t < SLOT, 0.0, origin)
    slot_ref[0] = origin_row.astype(jnp.int32) - 1
    slot_ref[1] = jnp.maximum(pltpu.roll(origin, SLOT, 1).astype(jnp.int32) - 1, 0)

    cond_ref = loaded(1)
    cond = [cond_ref[z] for z in range(layers)]
    all_delta, all_to = loaded(11)[...], loaded(13)[...]
    info = jnp.zeros((8, 128), f32)
    near_hot, next_hot = [], []
    for c in range(blocks):
        delta, to = all_delta[:, c : c + 1], all_to[:, c : c + 1]
        info = jnp.where(
            sub == c, jnp.where(lane < 64, delta.astype(f32), to.astype(f32)), info
        )
        near_hot.append(hot((block_of == c + delta) & (position == to)))
        next_hot.append(hot((block_of + blocks == c + delta) & (position == to)))
        inter_ref[c] = near_hot[c]
    put_halo(0, cond, info)
    pfrac_ref = loaded(3)

    pl.semaphore_wait(barrier, tiles - 1)
    for q in (*range(half // 8, tiles // 8), *range(half // 8)):
        put_eight(0, q, requests[8 * q : 8 * q + 8])
    start_halo(0)
    following = pltpu.make_async_remote_copy(
        src_ref=pfrac_ref,
        dst_ref=next_ref,
        send_sem=next_sem.at[0],
        recv_sem=next_sem.at[1],
        device_id=halo_to[0],
        device_id_type=LOGICAL,
    )
    following.start()

    all_from, all_trans = loaded(12)[...], loaded(14)[...]
    from_hot = jnp.zeros((8, 128), f32)
    for c in range(blocks):
        from_hot = jnp.where(
            (block_of == c) & (position == all_from[:, c : c + 1]),
            all_trans[:, c : c + 1],
            from_hot,
        )

    def later(x):
        moved = pltpu.roll(x, 127, 1)
        return jnp.where(lane == 127, pltpu.roll(moved, blocks, 0), moved)

    def earlier(x):
        moved = pltpu.roll(x, 1, 1)
        return jnp.where(lane == 0, pltpu.roll(moved, blocks, 0), moved)

    def chain(field, after, before):
        return after * later(field) + before * earlier(field)

    loaded(0)
    press = [press_ref[z] for z in range(layers)]
    press_f = folded(pfrac_ref[...])
    accum_f = folded(loaded(4)[...])
    t_next = jnp.where(position < block_len - 1, folded(loaded(5)[...]), 0.0)
    t_prev = jnp.where(position > 0, earlier(t_next), 0.0)
    coupling_mf = folded(loaded(6)[...])
    coupling_fm = folded(loaded(7)[...])
    diag_f = accum_f + t_next + t_prev + coupling_fm
    frac_ref[0] = t_next
    frac_ref[1] = t_prev
    frac_ref[2] = coupling_mf
    frac_ref[3] = coupling_fm
    frac_ref[4] = 1.0 / diag_f
    frac_ref[5] = from_hot

    well_tile, well_cell, well_rate = loaded(15)[...], loaded(16)[...], loaded(17)[...]
    wells = well_cell.shape[1]
    rate = jnp.where(well_tile == me, well_rate, 0.0)
    source = lax.dot_general(
        hot(iota((width_x, wells), 0) == well_cell // width_y) * rate,
        hot(iota((width_y, wells), 0) == well_cell % width_y),
        (((1,), (1,)), ((), ())),
        precision=lax.Precision.HIGHEST,
        preferred_element_type=f32,
    )
    accum_ref = loaded(2)
    put_halo(1, press, jnp.zeros((8, 128), f32))
    start_halo(1)

    halo = take_halo(0)
    along_y = gy * n_af + af
    inside = (
        (sub < 7) | (gx < n_gx - 1),
        (sub > 0) | (gx > 0),
        (lane < 127) | (along_y < n_gy * n_af - 1),
        (lane > 0) | (along_y > 0),
    )
    diag = []
    for z in range(layers):
        total = accum_ref[z]
        near = neighbours(cond, halo, z)
        for i in range(4):
            face = jnp.where(inside[i], harmonic(cond[z], near[i]), 0.0)
            trans_ref[i, z] = face
            total = total + face
        if z + 1 < layers:
            trans_ref[4, z] = 0.5 * harmonic(cond[z], cond[z + 1])
            total = total + trans_ref[4, z]
        if z > 0:
            total = total + trans_ref[4, z - 1]
        invm_ref[z] = 1.0 / total
        diag.append(total)
    for c in range(blocks):
        delta = halo[1][c : c + 1, 32:33].astype(jnp.int32)
        to = halo[1][c : c + 1, 64:65].astype(jnp.int32)
        inter_ref[blocks + c] = hot((block_of + blocks == c + delta) & (position == to))

    asked_here = take_all(0)
    first, second = asked_here[:half], asked_here[half:]
    want_row = jnp.where(left_half, first, pltpu.roll(second, SLOT, 1)).astype(jnp.int32) - 1
    want_col = jnp.where(left_half, pltpu.roll(first, SLOT, 1), second).astype(jnp.int32) - 1
    index_ref[0] = want_row
    index_ref[1] = jnp.maximum(want_col, 0)

    put_cross(1, press_ref, coupling_mf * press_f)
    for j in range(half):
        at = slice(128 * j, 128 * j + 128)
        rows_ref[:, at] = hot(
            iota((layers * width_x, 128), 0) == want_row[j : j + 1, :]
        ).astype(bf16)
        cols_ref[:, at] = hot(iota((width_y, 128), 0) == want_col[j : j + 1, :]).astype(bf16)

    following.wait_recv()
    next_f = folded(next_ref[...])
    crossing = jnp.zeros((8, 128), f32)
    for c in range(blocks):
        found = jnp.sum(near_hot[c] * press_f + next_hot[c] * next_f, axis=1, keepdims=True)
        found = jnp.sum(found, axis=0, keepdims=True)
        crossing = jnp.where(block_of == c, from_hot * found, crossing)

    def stencil(field, halo, z):
        near = neighbours(field, halo, z)
        total = trans_ref[0, z] * near[0]
        for i in range(1, 4):
            total = total + trans_ref[i, z] * near[i]
        if z + 1 < layers:
            total = total + trans_ref[4, z] * field[z + 1]
        if z > 0:
            total = total + trans_ref[4, z - 1] * field[z - 1]
        return total

    halo = take_halo(1)
    around = [stencil(press, halo, z) for z in range(layers)]
    cells, seg_values = take_cross(1)
    for z in range(layers):
        res = diag[z] * press[z] - around[z] - cells[z] - source
        resm_ref[z] = res
        adjm_ref[z] = res * invm_ref[z]
    res_f = diag_f * press_f - chain(press_f, t_next, t_prev) - coupling_fm * seg_values - crossing
    resf_ref[...] = unfolded(res_f)
    frac_ref[6] = res_f
    frac_ref[7] = res_f * frac_ref[4]

    def sweep(r, carry):
        field = [adjm_ref[z] for z in range(layers)]
        frac = frac_ref[7]
        sent = jnp.sum(frac_ref[5] * frac, axis=1, keepdims=True)
        sent = sent[:blocks] + sent[blocks:]
        put_cross(r, adjm_ref, frac_ref[3] * frac)
        put_halo(r, field, jnp.broadcast_to(jnp.concatenate([sent, sent], axis=0), (8, 128)))
        start_halo(r)
        total = frac_ref[6] + chain(frac, frac_ref[0], frac_ref[1])
        for c in range(blocks):
            total = total + inter_ref[c] * sent[c : c + 1, :]
        halo = take_halo(r)
        around = [resm_ref[z] + stencil(field, halo, z) for z in range(layers)]
        for c in range(blocks):
            total = total + inter_ref[blocks + c] * halo[1][c : c + 1, 64:65]
        cells, seg_values = take_cross(r)
        for z in range(layers):
            adjm_ref[z] = (around[z] + cells[z]) * invm_ref[z]
        frac_ref[7] = (total + frac_ref[2] * seg_values) * frac_ref[4]
        return carry

    lax.fori_loop(2, ROUNDS, sweep, 0)
    adjf_ref[...] = unfolded(frac_ref[7])

    following.wait_send()

    def finish(r, carry):
        wait_rows(send_ref, send_sem, r)
        for side in range(4):
            halo_copy(r, side).wait_send()
        return carry

    lax.fori_loop(0, ROUNDS, finish, 0)


def copy_out(*refs):
    sems = refs[8]
    copies = [pltpu.make_async_copy(refs[i], refs[4 + i], sems.at[i]) for i in range(4)]
    for copy in copies:
        copy.start()
    for copy in copies:
        copy.wait()


def body(sizes, *args):
    press_matrix, press_frac = args[0], args[3]
    args = list(args)
    for i in range(11, 18):
        args[i] = args[i].reshape(1, -1)
    tiles = sizes[0] * sizes[1] * sizes[2]
    layers, width_x, width_y = press_matrix.shape
    blocks, block_len = press_frac.shape
    slots = tiles * SLOT
    vmem = pl.BlockSpec(memory_space=pltpu.VMEM)
    anywhere = pl.BlockSpec(memory_space=pl.ANY)
    matrix = jax.ShapeDtypeStruct(press_matrix.shape, f32)
    fracture = jax.ShapeDtypeStruct(press_frac.shape, f32)
    out_shape = (matrix, fracture, matrix, fracture)
    results = pl.pallas_call(
        functools.partial(kernel, sizes),
        out_shape=tuple(pltpu.VMEM(x.shape, f32) for x in out_shape),
        in_specs=[anywhere] * 18,
        out_specs=(vmem,) * 4,
        scratch_shapes=[pltpu.VMEM(x.shape, x.dtype) for x in args]
        + [
            pltpu.VMEM((5, layers, width_x, width_y), f32),
            pltpu.VMEM((layers, width_x, width_y), f32),
            pltpu.VMEM((8, 8, 128), f32),
            pltpu.VMEM((2 * blocks, 8, 128), f32),
            pltpu.VMEM((width_y, slots), bf16),
            pltpu.VMEM((layers * width_x, slots), bf16),
            pltpu.VMEM((2, tiles // 2, 128), jnp.int32),
            pltpu.VMEM((2, tiles, 128), jnp.int32),
            pltpu.VMEM((2, 8, 128), jnp.int32),
            pltpu.VMEM((ROUNDS, tiles, 1, 128), f32),
            pltpu.VMEM((ROUNDS, tiles, 1, 128), f32),
            pltpu.VMEM((ROUNDS, 4, 8, 128), f32),
            pltpu.VMEM((ROUNDS, 4, 8, 128), f32),
            pltpu.VMEM((blocks, block_len), f32),
            pltpu.SemaphoreType.DMA((18,)),
            pltpu.SemaphoreType.DMA((ROUNDS,)),
            pltpu.SemaphoreType.DMA((ROUNDS,)),
            pltpu.SemaphoreType.DMA((ROUNDS, 4)),
            pltpu.SemaphoreType.DMA((ROUNDS, 4)),
            pltpu.SemaphoreType.DMA((2,)),
        ],
        compiler_params=pltpu.CompilerParams(
            collective_id=0, has_side_effects=True, vmem_limit_bytes=60 * 1024 * 1024
        ),
    )(*args)
    return pl.pallas_call(
        copy_out,
        out_shape=out_shape,
        in_specs=[vmem] * 4,
        out_specs=(anywhere,) * 4,
        scratch_shapes=[pltpu.SemaphoreType.DMA((4,))],
        compiler_params=pltpu.CompilerParams(vmem_limit_bytes=4 * 1024 * 1024),
    )(*results)


def solution(mesh):
    slab = P(None, "gx", ("gy", "af"))
    fracture = P(("gx", "gy", "af"), None)
    block = P(("gx", "gy", "af"))
    in_specs = (slab,) * 3 + (fracture,) * 8 + (block,) * 4 + (P(),) * 3
    out_specs = (slab, fracture, slab, fracture)
    sizes = tuple(mesh.shape[axis] for axis in ("gx", "gy", "af"))
    return jax.shard_map(
        functools.partial(body, sizes),
        mesh=mesh,
        in_specs=in_specs,
        out_specs=out_specs,
        check_vma=False,
    )
```

```python
import functools

import jax
import jax.numpy as jnp
from jax import lax
from jax.experimental import pallas as pl
from jax.experimental.pallas import tpu as pltpu
from jax.sharding import PartitionSpec as P

ITERS = 8
ROUNDS = ITERS + 1
SLOT = 64
LOGICAL = pl.DeviceIdType.LOGICAL
f32 = jnp.float32
bf16 = jnp.bfloat16


def harmonic(first, second):
    return 2.0 * first * second / (first + second)


def iota(shape, dim):
    return lax.broadcasted_iota(jnp.int32, shape, dim)


def hot(mask):
    return jnp.where(mask, 1.0, 0.0)


def pieces(values):
    high = values.astype(bf16)
    return high, (values - high.astype(f32)).astype(bf16)


def dot_nn(a, b):
    return lax.dot_general(a, b, (((1,), (0,)), ((), ())), preferred_element_type=f32)


def dot_nt(a, b):
    return lax.dot_general(a, b, (((1,), (1,)), ((), ())), preferred_element_type=f32)


def taken(row, lanes):
    return jnp.take_along_axis(
        jnp.broadcast_to(row, lanes.shape), lanes, axis=1, mode="promise_in_bounds"
    )


def by_eight(x):
    return [x[8 * q : 8 * q + 8] for q in range(x.shape[0] // 8)]


def kernel(sizes, *refs):
    hbm, outs, held, rest = refs[:18], refs[18:22], refs[22:40], refs[40:]
    resm_ref, resf_ref, adjm_ref, adjf_ref = outs
    (
        trans_ref,
        invm_ref,
        frac_ref,
        inter_ref,
        cols_ref,
        rows_ref,
        index_ref,
        slot_ref,
        seg_ref,
        send_ref,
        stage_ref,
        mid_ref,
        pass_ref,
        recv_ref,
        hsend_ref,
        hrecv_ref,
        next_ref,
        load_sem,
        send_sem,
        mid_sem,
        pass_sem,
        recv_sem,
        hsend_sem,
        hrecv_sem,
        next_sem,
    ) = rest
    n_gx, n_gy, n_af = sizes
    tiles = n_gx * n_gy * n_af
    half = tiles // 2
    gx, gy, af = lax.axis_index("gx"), lax.axis_index("gy"), lax.axis_index("af")
    planes = n_gx * n_gy
    plane = gx * n_gy + gy
    me = plane * n_af + af
    barrier = pltpu.get_barrier_semaphore()

    loads = [pltpu.make_async_copy(hbm[i], held[i], load_sem.at[i]) for i in range(18)]
    for i in (8, 9, 10, 1, 11, 13, 3, 12, 14, 0, 4, 5, 6, 7, 15, 16, 17, 2):
        loads[i].start()

    def wrapped(k):
        return lax.rem(me + k, tiles)

    beside = [plane * n_af + lax.rem(af + k, n_af) for k in range(n_af)]
    across = [wrapped(k * n_af) for k in range(planes)]
    for k in range(1, tiles):
        pl.semaphore_signal(
            barrier, inc=1, device_id=wrapped(k), device_id_type=LOGICAL
        )

    def loaded(i):
        loads[i].wait()
        return held[i]

    press_ref, cond_ref = held[0], held[1]
    layers, width_x, width_y = press_ref.shape
    blocks, block_len = held[3].shape

    lane = iota((8, 128), 1)
    sub = iota((8, 128), 0)
    block_of = sub % blocks
    position = lane + 128 * (sub // blocks)
    row_t = iota((tiles, 128), 0)
    lane_t = iota((tiles, 128), 1)
    left_half = iota((half, 128), 1) < SLOT

    def folded(x):
        return jnp.concatenate([x[:, :128], x[:, 128:]], axis=0)

    def unfolded(x):
        return jnp.concatenate([x[:blocks], x[blocks:]], axis=1)

    halo_to = (
        wrapped(tiles - 1),
        wrapped(1),
        wrapped(tiles - n_gy * n_af),
        wrapped(n_gy * n_af),
    )

    def halo_copy(r, side):
        return pltpu.make_async_remote_copy(
            src_ref=hsend_ref.at[r, side],
            dst_ref=hrecv_ref.at[r, side],
            send_sem=hsend_sem.at[r, side],
            recv_sem=hrecv_sem.at[r, side],
            device_id=halo_to[side],
            device_id_type=LOGICAL,
        )

    def put_halo(r, field, extra):
        low = jnp.zeros((8, 128), f32)
        high = extra
        for z in range(layers):
            at = lane == z
            low = jnp.where(at, field[z] if z == 0 else pltpu.roll(field[z], z, 1), low)
            high = jnp.where(at, pltpu.roll(field[z], z + 1, 1), high)
        hsend_ref[r, 0] = low
        hsend_ref[r, 1] = high
        hsend_ref[r, 2] = jnp.concatenate([m[0:1, :] for m in field], axis=0)
        hsend_ref[r, 3] = jnp.concatenate([m[7:8, :] for m in field], axis=0)

    def start_halo(r):
        for side in range(4):
            halo_copy(r, side).start()

    def take_halo(r):
        for side in range(4):
            halo_copy(r, side).wait_recv()
        return [hrecv_ref[r, side] for side in range(4)]

    def neighbours(field, halo, z):
        m = field[z]
        after, before, above, below = halo
        y_up = jnp.where(lane == 127, pltpu.roll(after, 127 - z, 1), pltpu.roll(m, 127, 1))
        shifted = before if z == 0 else pltpu.roll(before, 128 - z, 1)
        y_down = jnp.where(lane == 0, shifted, pltpu.roll(m, 1, 1))
        x_up = jnp.where(sub == 7, above[z : z + 1, :], pltpu.roll(m, 7, 0))
        x_down = jnp.where(sub == 0, below[z : z + 1, :], pltpu.roll(m, 1, 0))
        return x_up, x_down, y_up, y_down

    def put_rows(r, message):
        for q in range(tiles // 8):
            stage_ref[8 * q : 8 * q + 8] = message[q].reshape(8, 1, 128)
        for p in range(tiles):
            i, j = p % n_af, p // n_af
            row = stage_ref[p]
            if i > 0:
                send_ref[r, i * planes + j] = row
            elif j > 0:
                pass_ref[r, j * n_af] = row
            else:
                recv_ref[r, 0] = row
        for i in range(1, n_af):
            pltpu.make_async_remote_copy(
                src_ref=send_ref.at[r, pl.ds(i * planes, planes)],
                dst_ref=mid_ref.at[r, pl.ds((n_af - i) * planes, planes)],
                send_sem=send_sem.at[r],
                recv_sem=mid_sem.at[r],
                device_id=beside[i],
                device_id_type=LOGICAL,
            ).start()

    def wait_rows(ref, sem, r, own):
        part = ref.at[r, pl.ds(own, tiles - own)]
        pltpu.make_async_copy(part, part, sem.at[r]).wait()

    def pass_on(r):
        wait_rows(mid_ref, mid_sem, r, planes)
        for i in range(1, n_af):
            recv_ref[r, i] = mid_ref[r, i * planes]
        for j in range(1, planes):
            for i in range(1, n_af):
                pass_ref[r, j * n_af + i] = mid_ref[r, i * planes + j]
        for j in range(1, planes):
            pltpu.make_async_remote_copy(
                src_ref=pass_ref.at[r, pl.ds(j * n_af, n_af)],
                dst_ref=recv_ref.at[r, pl.ds((planes - j) * n_af, n_af)],
                send_sem=pass_sem.at[r],
                recv_sem=recv_sem.at[r],
                device_id=across[j],
                device_id_type=LOGICAL,
            ).start()

    def take_all(r):
        wait_rows(recv_ref, recv_sem, r, n_af)
        return recv_ref[r][:, 0, :]

    def put_cross(r, field_ref, weights):
        rows = [jnp.broadcast_to(weights[i : i + 1, :], (8, 128)) for i in range(8)]
        message = [None] * (tiles // 8)
        for q in range(half // 8):
            at_row = index_ref[0, 8 * q : 8 * q + 8]
            at_lane = index_ref[1, 8 * q : 8 * q + 8]
            wanted = jnp.zeros((8, 128), f32)
            for z in range(layers):
                for x in range(width_x):
                    got = taken(field_ref[z, x : x + 1, :], at_lane)
                    wanted = jnp.where(at_row == z * width_x + x, got, wanted)
            for p, values in ((q + half // 8, pltpu.roll(wanted, SLOT, 1)), (q, wanted)):
                at_row = slot_ref[0, 8 * p : 8 * p + 8]
                at_lane = slot_ref[1, 8 * p : 8 * p + 8]
                found = jnp.zeros((8, 128), f32)
                for i in range(8):
                    found = jnp.where(at_row == i, taken(rows[i], at_lane), found)
                message[p] = jnp.where(lane < SLOT, values, found)
        put_rows(r, message)

    def take_cross(r):
        message = take_all(r)
        incoming = jnp.where(left_half, pltpu.roll(message[:half], SLOT, 1), message[half:])
        high, low = pieces(incoming)
        parts = []
        for piece in (high.astype(f32), low.astype(f32)):
            scaled = []
            for j in range(half):
                one = jnp.broadcast_to(piece[j : j + 1, :], (16, 128)).astype(bf16)
                wide = jnp.concatenate([one] * (layers * width_x // 16), axis=0)
                scaled.append(rows_ref[:, 128 * j : 128 * j + 128] * wide)
            parts.append(jnp.concatenate(scaled, axis=1))
        both = dot_nt(jnp.concatenate(parts, axis=0), cols_ref[...])
        cells = both[: layers * width_x] + both[layers * width_x :]
        of, rank = seg_ref[0], seg_ref[1]
        seg_values = jnp.zeros((8, 128), f32)
        for t in range(tiles):
            seg_values = jnp.where(of == t, taken(recv_ref[r, t], rank), seg_values)
        return [cells[8 * z : 8 * z + 8] for z in range(layers)], seg_values

    owner = folded(loaded(8)[...])
    ahead = owner // n_af - plane
    ahead = jnp.where(ahead < 0, ahead + planes, ahead)
    along = owner % n_af - af
    along = jnp.where(along < 0, along + n_af, along)
    owner = ahead * n_af + along
    layer = folded(loaded(9)[...])
    cell = folded(loaded(10)[...])
    cell_row = (layer * width_x + cell // width_y).astype(f32) + 1.0
    cell_col = (cell % width_y).astype(f32) + 1.0
    owner_hot = [hot(row_t == owner[g : g + 1, :]) for g in range(8)]
    tri_row = iota((128, 256), 0)
    tri_col = iota((128, 256), 1)
    counted = dot_nn(
        jnp.concatenate(owner_hot, axis=0).astype(bf16),
        hot((tri_row < tri_col) | (tri_col >= 128)).astype(bf16),
    )
    base = jnp.zeros((tiles, 128), f32)
    ranks = []
    for g in range(8):
        part = counted[g * tiles : (g + 1) * tiles]
        ranks.append(jnp.sum(owner_hot[g] * (part[:, :128] + base), axis=0, keepdims=True))
        base = base + part[:, 128:]
    rank = jnp.concatenate(ranks, axis=0).astype(jnp.int32)
    seg_ref[0] = owner
    seg_ref[1] = rank
    slot = iota((128, 128), 0)
    lane_up = iota((128, 128), 1).astype(f32) + 1.0
    asked, origin = [], []
    for g in range(8):
        low = slot == rank[g : g + 1, :]
        high = slot == rank[g : g + 1, :] + SLOT
        asked.append(
            jnp.where(low, cell_row[g : g + 1, :], jnp.where(high, cell_col[g : g + 1, :], 0.0))
        )
        origin.append(jnp.where(low, lane_up, jnp.where(high, g + 1.0, 0.0)))
    table = jnp.concatenate(
        [jnp.concatenate(asked, axis=1), jnp.concatenate(origin, axis=1)], axis=0
    )
    spread = dot_nt(jnp.concatenate(owner_hot, axis=1).astype(bf16), table.astype(bf16))
    requests = spread[:, :128]
    origin = spread[:, 128:]
    origin_row = jnp.where(lane_t < SLOT, 0.0, origin)
    slot_ref[0] = origin_row.astype(jnp.int32) - 1
    slot_ref[1] = jnp.maximum(pltpu.roll(origin, SLOT, 1).astype(jnp.int32) - 1, 0)

    cond_ref = loaded(1)
    cond = [cond_ref[z] for z in range(layers)]
    all_delta, all_to = loaded(11)[...], loaded(13)[...]
    info = jnp.zeros((8, 128), f32)
    near_hot, next_hot = [], []
    for c in range(blocks):
        delta, to = all_delta[:, c : c + 1], all_to[:, c : c + 1]
        info = jnp.where(
            sub == c, jnp.where(lane < 64, delta.astype(f32), to.astype(f32)), info
        )
        near_hot.append(hot((block_of == c + delta) & (position == to)))
        next_hot.append(hot((block_of + blocks == c + delta) & (position == to)))
        inter_ref[c] = near_hot[c]
    put_halo(0, cond, info)
    pfrac_ref = loaded(3)

    pl.semaphore_wait(barrier, tiles - 1)
    put_rows(0, by_eight(requests))
    start_halo(0)
    following = pltpu.make_async_remote_copy(
        src_ref=pfrac_ref,
        dst_ref=next_ref,
        send_sem=next_sem.at[0],
        recv_sem=next_sem.at[1],
        device_id=halo_to[0],
        device_id_type=LOGICAL,
    )
    following.start()
    pass_on(0)

    all_from, all_trans = loaded(12)[...], loaded(14)[...]
    from_hot = jnp.zeros((8, 128), f32)
    for c in range(blocks):
        from_hot = jnp.where(
            (block_of == c) & (position == all_from[:, c : c + 1]),
            all_trans[:, c : c + 1],
            from_hot,
        )

    def later(x):
        moved = pltpu.roll(x, 127, 1)
        return jnp.where(lane == 127, pltpu.roll(moved, blocks, 0), moved)

    def earlier(x):
        moved = pltpu.roll(x, 1, 1)
        return jnp.where(lane == 0, pltpu.roll(moved, blocks, 0), moved)

    def chain(field, after, before):
        return after * later(field) + before * earlier(field)

    loaded(0)
    press = [press_ref[z] for z in range(layers)]
    press_f = folded(pfrac_ref[...])
    accum_f = folded(loaded(4)[...])
    t_next = jnp.where(position < block_len - 1, folded(loaded(5)[...]), 0.0)
    t_prev = jnp.where(position > 0, earlier(t_next), 0.0)
    coupling_mf = folded(loaded(6)[...])
    coupling_fm = folded(loaded(7)[...])
    diag_f = accum_f + t_next + t_prev + coupling_fm
    frac_ref[0] = t_next
    frac_ref[1] = t_prev
    frac_ref[2] = coupling_mf
    frac_ref[3] = coupling_fm
    frac_ref[4] = 1.0 / diag_f
    frac_ref[5] = from_hot

    well_tile, well_cell, well_rate = loaded(15)[...], loaded(16)[...], loaded(17)[...]
    wells = well_cell.shape[1]
    rate = jnp.where(well_tile == me, well_rate, 0.0)
    source = lax.dot_general(
        hot(iota((width_x, wells), 0) == well_cell // width_y) * rate,
        hot(iota((width_y, wells), 0) == well_cell % width_y),
        (((1,), (1,)), ((), ())),
        precision=lax.Precision.HIGHEST,
        preferred_element_type=f32,
    )
    accum_ref = loaded(2)

    halo = take_halo(0)
    along_y = gy * n_af + af
    inside = (
        (sub < 7) | (gx < n_gx - 1),
        (sub > 0) | (gx > 0),
        (lane < 127) | (along_y < n_gy * n_af - 1),
        (lane > 0) | (along_y > 0),
    )
    diag = []
    for z in range(layers):
        total = accum_ref[z]
        near = neighbours(cond, halo, z)
        for i in range(4):
            face = jnp.where(inside[i], harmonic(cond[z], near[i]), 0.0)
            trans_ref[i, z] = face
            total = total + face
        if z + 1 < layers:
            trans_ref[4, z] = 0.5 * harmonic(cond[z], cond[z + 1])
            total = total + trans_ref[4, z]
        if z > 0:
            total = total + trans_ref[4, z - 1]
        invm_ref[z] = 1.0 / total
        diag.append(total)
    for c in range(blocks):
        delta = halo[1][c : c + 1, 32:33].astype(jnp.int32)
        to = halo[1][c : c + 1, 64:65].astype(jnp.int32)
        inter_ref[blocks + c] = hot((block_of + blocks == c + delta) & (position == to))

    asked_here = take_all(0)
    first, second = asked_here[:half], asked_here[half:]
    want_row = jnp.where(left_half, first, pltpu.roll(second, SLOT, 1)).astype(jnp.int32) - 1
    want_col = jnp.where(left_half, pltpu.roll(first, SLOT, 1), second).astype(jnp.int32) - 1
    index_ref[0] = want_row
    index_ref[1] = jnp.maximum(want_col, 0)

    put_cross(1, press_ref, coupling_mf * press_f)
    put_halo(1, press, jnp.zeros((8, 128), f32))
    start_halo(1)
    pass_on(1)
    for j in range(half):
        at = slice(128 * j, 128 * j + 128)
        rows_ref[:, at] = hot(
            iota((layers * width_x, 128), 0) == want_row[j : j + 1, :]
        ).astype(bf16)
        cols_ref[:, at] = hot(iota((width_y, 128), 0) == want_col[j : j + 1, :]).astype(bf16)

    following.wait_recv()
    next_f = folded(next_ref[...])
    crossing = jnp.zeros((8, 128), f32)
    for c in range(blocks):
        found = jnp.sum(near_hot[c] * press_f + next_hot[c] * next_f, axis=1, keepdims=True)
        found = jnp.sum(found, axis=0, keepdims=True)
        crossing = jnp.where(block_of == c, from_hot * found, crossing)

    def stencil(field, halo, z):
        near = neighbours(field, halo, z)
        total = trans_ref[0, z] * near[0]
        for i in range(1, 4):
            total = total + trans_ref[i, z] * near[i]
        if z + 1 < layers:
            total = total + trans_ref[4, z] * field[z + 1]
        if z > 0:
            total = total + trans_ref[4, z - 1] * field[z - 1]
        return total

    halo = take_halo(1)
    around = [stencil(press, halo, z) for z in range(layers)]
    cells, seg_values = take_cross(1)
    for z in range(layers):
        res = diag[z] * press[z] - around[z] - cells[z] - source
        resm_ref[z] = res
        adjm_ref[z] = res * invm_ref[z]
    res_f = diag_f * press_f - chain(press_f, t_next, t_prev) - coupling_fm * seg_values - crossing
    resf_ref[...] = unfolded(res_f)
    frac_ref[6] = res_f
    frac_ref[7] = res_f * frac_ref[4]

    def sweep(r, carry):
        field = [adjm_ref[z] for z in range(layers)]
        frac = frac_ref[7]
        sent = jnp.sum(frac_ref[5] * frac, axis=1, keepdims=True)
        sent = sent[:blocks] + sent[blocks:]
        put_cross(r, adjm_ref, frac_ref[3] * frac)
        put_halo(r, field, jnp.broadcast_to(jnp.concatenate([sent, sent], axis=0), (8, 128)))
        start_halo(r)
        pass_on(r)
        total = frac_ref[6] + chain(frac, frac_ref[0], frac_ref[1])
        for c in range(blocks):
            total = total + inter_ref[c] * sent[c : c + 1, :]
        halo = take_halo(r)
        around = [resm_ref[z] + stencil(field, halo, z) for z in range(layers)]
        for c in range(blocks):
            total = total + inter_ref[blocks + c] * halo[1][c : c + 1, 64:65]
        cells, seg_values = take_cross(r)
        for z in range(layers):
            adjm_ref[z] = (around[z] + cells[z]) * invm_ref[z]
        frac_ref[7] = (total + frac_ref[2] * seg_values) * frac_ref[4]
        return carry

    lax.fori_loop(2, ROUNDS, sweep, 0)
    adjf_ref[...] = unfolded(frac_ref[7])

    following.wait_send()

    def finish(r, carry):
        wait_rows(send_ref, send_sem, r, planes)
        wait_rows(pass_ref, pass_sem, r, n_af)
        for side in range(4):
            halo_copy(r, side).wait_send()
        return carry

    lax.fori_loop(0, ROUNDS, finish, 0)


def copy_out(*refs):
    sems = refs[8]
    copies = [pltpu.make_async_copy(refs[i], refs[4 + i], sems.at[i]) for i in range(4)]
    for copy in copies:
        copy.start()
    for copy in copies:
        copy.wait()


def body(sizes, *args):
    press_matrix, press_frac = args[0], args[3]
    args = list(args)
    for i in range(11, 18):
        args[i] = args[i].reshape(1, -1)
    planes, n_af = sizes[0] * sizes[1], sizes[2]
    tiles = planes * n_af
    layers, width_x, width_y = press_matrix.shape
    blocks, block_len = press_frac.shape
    slots = tiles * SLOT
    vmem = pl.BlockSpec(memory_space=pltpu.VMEM)
    anywhere = pl.BlockSpec(memory_space=pl.ANY)
    matrix = jax.ShapeDtypeStruct(press_matrix.shape, f32)
    fracture = jax.ShapeDtypeStruct(press_frac.shape, f32)
    out_shape = (matrix, fracture, matrix, fracture)
    results = pl.pallas_call(
        functools.partial(kernel, sizes),
        out_shape=tuple(pltpu.VMEM(x.shape, f32) for x in out_shape),
        in_specs=[anywhere] * 18,
        out_specs=(vmem,) * 4,
        scratch_shapes=[pltpu.VMEM(x.shape, x.dtype) for x in args]
        + [
            pltpu.VMEM((5, layers, width_x, width_y), f32),
            pltpu.VMEM((layers, width_x, width_y), f32),
            pltpu.VMEM((8, 8, 128), f32),
            pltpu.VMEM((2 * blocks, 8, 128), f32),
            pltpu.VMEM((width_y, slots), bf16),
            pltpu.VMEM((layers * width_x, slots), bf16),
            pltpu.VMEM((2, tiles // 2, 128), jnp.int32),
            pltpu.VMEM((2, tiles, 128), jnp.int32),
            pltpu.VMEM((2, 8, 128), jnp.int32),
            pltpu.VMEM((ROUNDS, tiles, 1, 128), f32),
            pltpu.VMEM((tiles, 1, 128), f32),
            pltpu.VMEM((ROUNDS, tiles, 1, 128), f32),
            pltpu.VMEM((ROUNDS, tiles, 1, 128), f32),
            pltpu.VMEM((ROUNDS, tiles, 1, 128), f32),
            pltpu.VMEM((ROUNDS, 4, 8, 128), f32),
            pltpu.VMEM((ROUNDS, 4, 8, 128), f32),
            pltpu.VMEM((blocks, block_len), f32),
            pltpu.SemaphoreType.DMA((18,)),
            pltpu.SemaphoreType.DMA((ROUNDS,)),
            pltpu.SemaphoreType.DMA((ROUNDS,)),
            pltpu.SemaphoreType.DMA((ROUNDS,)),
            pltpu.SemaphoreType.DMA((ROUNDS,)),
            pltpu.SemaphoreType.DMA((ROUNDS, 4)),
            pltpu.SemaphoreType.DMA((ROUNDS, 4)),
            pltpu.SemaphoreType.DMA((2,)),
        ],
        compiler_params=pltpu.CompilerParams(
            collective_id=0, has_side_effects=True, vmem_limit_bytes=60 * 1024 * 1024
        ),
    )(*args)
    return pl.pallas_call(
        copy_out,
        out_shape=out_shape,
        in_specs=[vmem] * 4,
        out_specs=(anywhere,) * 4,
        scratch_shapes=[pltpu.SemaphoreType.DMA((4,))],
        compiler_params=pltpu.CompilerParams(vmem_limit_bytes=4 * 1024 * 1024),
    )(*results)


def solution(mesh):
    slab = P(None, "gx", ("gy", "af"))
    fracture = P(("gx", "gy", "af"), None)
    block = P(("gx", "gy", "af"))
    in_specs = (slab,) * 3 + (fracture,) * 8 + (block,) * 4 + (P(),) * 3
    out_specs = (slab, fracture, slab, fracture)
    sizes = tuple(mesh.shape[axis] for axis in ("gx", "gy", "af"))
    return jax.shard_map(
        functools.partial(body, sizes),
        mesh=mesh,
        in_specs=in_specs,
        out_specs=out_specs,
        check_vma=False,
    )
```
